256 devices in a mesh: vol: 8 (over z_lo, y), gz: 32 (over x, z_hi, core).
Axes of the slice: x: 4, y: 4, z: 8 (z_hi: 4, z_lo: 2; z = z_hi * 2 + z_lo), core: 2. Of those that a mesh axis runs over, the one named last changes fastest.
Arguments:
- volume: bfloat16 [8, 32, 128, 64, 128], P('vol', None, 'gz'), may hold values from -6 to 6
- kernel: bfloat16 [64, 32, 3, 3, 3], replicated, may hold values from -0.21875 to 0.21875
- cotangent: bfloat16 [8, 64, 64, 32, 64], P('vol', None, None, 'gz'), may hold values from -6 to 6
Outputs:
- features: bfloat16 [8, 64, 64, 32, 64], P('vol', None, None, 'gz')
- volume_grad: bfloat16 [8, 32, 128, 64, 128], P('vol', None, 'gz')
- kernel_grad: float32 [64, 32, 3, 3, 3], replicated
The draws below stay inside these ranges and needn't reach their ends.
All inputs are finite; a program needn't handle non-finite values.
Results may differ from the reference program's by a relative error of at most 0.004.
Values may be sent and summed in bfloat16 or wider, within the bound.
A program may use at most 192 MiB of HBM per device.

```python
import jax
import jax.numpy as jnp
from jax import lax

CIN = 32
COUT = 64
Y = 64
X = 128
VOLUMES = 8
Z = 128
OZ = 64
OY = 32
OX = 64


def level_of(own_key, shape, pieces, least, high):
    loudness, own = 1.0, jax.random.fold_in(own_key, 6)
    for position, parts in pieces:
        heights = jnp.exp(jax.random.uniform(jax.random.fold_in(own, position), (parts,), jnp.float32, least / len(pieces), high / len(pieces)))
        loudness = loudness * jnp.repeat(heights, shape[position] // parts).reshape([-1 if axis == position else 1 for axis in range(len(shape))])
    return loudness


def centred(key, shape, spread, reach, pieces=(), held_as=jnp.bfloat16):
    array = spread * jax.random.normal(key, shape, jnp.float32)
    if pieces:
        array = array * level_of(key, shape, pieces, -0.22, 0.18)
    return jnp.clip(array, -reach, reach).astype(held_as)


def setup_inputs(seed: int = 0) -> dict:
    seeds = jax.random.split(jax.random.key(seed), 4)
    volume = centred(seeds[0], (VOLUMES, CIN, Z, Y, X), 1.0, 6.0, ((0, 8), (2, 32)))
    kernel = centred(seeds[1], (COUT, CIN, 3, 3, 3), (CIN * 27) ** -0.5, 0.21875)
    cotangent = centred(seeds[2], (VOLUMES, COUT, OZ, OY, OX), 1.0, 6.0, ((0, 8), (3, 32)))
    return dict(volume=volume, kernel=kernel, cotangent=cotangent)


def convolve(volume_one, kernel_one):
    return lax.conv_general_dilated(volume_one[None], kernel_one, (2, 2, 2), ((1, 1), (1, 1), (1, 1)), dimension_numbers=('NCDHW', 'OIDHW', 'NCDHW'), precision=lax.Precision.HIGHEST)[0]

def reference(volume, kernel, cotangent):
    kernel_wide = kernel.astype(jnp.float32)

    def one_volume(carry, pair):
        volume_one, grads_one = pair
        output, pullback = jax.vjp(convolve, volume_one.astype(jnp.float32), kernel_wide)
        input_grad, weight_grad = pullback(grads_one.astype(jnp.float32))
        return (carry + weight_grad, (output.astype(jnp.bfloat16), input_grad.astype(jnp.bfloat16)))
    start = jnp.zeros(kernel.shape, jnp.float32)
    summed, (features, volume_grad) = lax.scan(one_volume, start, (volume, cotangent))
    return (features, volume_grad, summed / VOLUMES)
```

```python
import functools

import jax
import jax.numpy as jnp
import numpy as np
from jax import lax
from jax.experimental import pallas as pl
from jax.experimental.pallas import tpu as pltpu
from jax.sharding import PartitionSpec as P

MESH = pl.DeviceIdType.MESH
BF = jnp.bfloat16
F32 = jnp.float32

CI, CO, SLABS, BANDS = 32, 64, 32, 4
QB = 5 * CO

BACK = ((0, 0), (0, 2), (2, 2), (2, 0), (0, 1), (2, 1), (1, 2), (1, 0), (1, 1))
FRONT = ((1, 0), (1, 1), (1, 2), (2, 0), (2, 1), (2, 2), (0, 0), (0, 1), (0, 2))
TAPS = tuple((a, b, e) for e in range(3) for a in (1, 2, 0) for b in range(3))
GROUPS = 7


def one_hot(rows, columns, test):
    row, column = np.meshgrid(np.arange(rows), np.arange(columns), indexing="ij")
    return np.asarray(test(row, column), np.float32).astype(jnp.bfloat16)


def pair_pick(row, column):
    half, o, p = column // 256, column // 16 % 16, column % 16
    return (row % 16 == o) & (p == 2 * (row // 16) + half)


def even_pick(row, column):
    o, p = column // 16 % 16, column % 16
    return (row % 16 == o) & (p == 2 * (row // 16))


def unpick(row, column):
    half, slab, o = column // 128, column // 16 % 8, column % 16
    return (row // 16 == o) & (row % 16 == 2 * slab + half)


def place(row, column):
    ql, c, yl = row // 256, row // 8 % 32, row % 8
    b, channel = column // 32, column % 32
    return (b < 3) & (c == channel) & (yl == 2 * ql + b - 1)


def spread_x(row, column):
    zz, x = row // 128, row % 128
    e, half, r = column // 128, column // 64 % 2, column % 64
    return (zz == half) & (x == 2 * r + e - 1)


def weave_x(row, column):
    parity, zz, r = row // 128, row // 64 % 2, row % 64
    return (zz == column // 128) & (column % 128 == 2 * r + parity)


def later_planes(high, row, column):
    kind, lane = column // 128, column % 128
    shift = np.where(kind == 1, 0, 1)
    valid = (lane % 64 + shift) < 64
    lane = lane + shift
    later = np.where(lane % 128 < 64, lane + 64, 128 + lane - (0 if high else 64))
    return valid & (row == np.where(kind == 2, lane, later))


def halves(row, column):
    return (column % 64 == row) & ((column // 64 == 0) | (column // 64 == 3))


def join(upper, row, column):
    even = (row == column) | (row == 128 + 64 * upper + column)
    odd = row == column - 64
    return np.where(column < 64, even, (column // 64 == 2) & odd)


def sum_band(row, column):
    return row // 8 == column


CONSTANTS = (
    ("halves", one_hot(64, 256, halves)),
    ("pairs", one_hot(128, 512, pair_pick)),
    ("evens", one_hot(128, 512, even_pick)),
    ("place", one_hot(5 * 256, 128, place)),
    ("place_t", np.ascontiguousarray(one_hot(5 * 256, 128, place).T)),
    ("spread", one_hot(256, 384, spread_x)),
    ("later_lo", one_hot(256, 384, functools.partial(later_planes, False))),
    ("later_hi", one_hot(256, 384, functools.partial(later_planes, True))),
    ("bands", one_hot(1024, 128, sum_band)),
    ("weave", one_hot(256, 256, weave_x)),
    ("join_lo", one_hot(256, 256, functools.partial(join, 0))),
    ("join_hi", one_hot(256, 256, functools.partial(join, 1))),
    ("unpick", one_hot(256, 256, unpick)),
)
NC = len(CONSTANTS)


def dot(a, b):
    return jnp.dot(a, b, preferred_element_type=F32)


def dot_nt(a, b):
    return lax.dot_general(a, b, (((1,), (1,)), ((), ())), preferred_element_type=F32)


def kernel(*refs):
    (vol_in, w_in, cot_in), refs = refs[:3], refs[3:]
    const_in, refs = refs[:NC], refs[NC:]
    (feat_out, vgrad_out, kgrad_out), refs = refs[:3], refs[3:]
    const, refs = refs[:NC], refs[NC:]
    k = {name: ref for (name, _), ref in zip(CONSTANTS, const)}
    (vol, w, cot, feat, vgrad, kgrad, cs, cr, fs, rf, wa, tc, tt_oo, tt_oe, tt_e, vc, c4,
     carry, dh, dl, p1, r1, s1, r2, s2, r3, s3, r4, r5,
     in_sem, const_sem, out_sem, cot_send, cot_recv, ft_send, ft_recv,
     a_send, a_recv, z_send, z_recv, x_send, x_recv, zz_send, zz_recv, aa_send, aa_recv) = refs

    mv, mg = lax.axis_index("vol"), lax.axis_index("gz")
    y, z_lo = mv % 4, mv // 4
    core, z_hi, x = mg % 2, mg // 2 % 4, mg // 8
    mine, z = y * 2 + core, z_hi * 2 + z_lo

    barrier = pltpu.get_barrier_semaphore()

    def greet(v, g):
        pl.semaphore_signal(barrier, inc=1, device_id=(v, g), device_id_type=MESH)

    def greet_slab(i, _):
        greet(mv, (mg + i) % SLABS)
        return 0

    lax.fori_loop(1, SLABS, greet_slab, 0)
    for step in range(1, 4):
        for other in range(2):
            greet(z_lo * 4 + (y + step) % 4, mg - core + other)
    for other in range(4):
        greet((1 - z_lo) * 4 + y, x * 8 + other * 2 + core)

    load_cot = pltpu.make_async_copy(cot_in, cot, in_sem.at[0])
    load_w = pltpu.make_async_copy(w_in, w, in_sem.at[1])
    load_vol = pltpu.make_async_copy(vol_in, vol, in_sem.at[2])
    loads = {
        name: pltpu.make_async_copy(const_in[i], const[i], const_sem.at[i])
        for i, (name, _) in enumerate(CONSTANTS)
    }
    load_cot.start()
    for name in ("halves", "pairs", "evens"):
        loads[name].start()
    load_w.start()
    load_vol.start()
    for name in list(loads)[3:]:
        loads[name].start()

    cs[SLABS, 64:96, :] = jnp.zeros((32, 128), BF)
    rf[0, 64:96, :] = jnp.zeros((32, 128), BF)
    c4[BANDS, 1024:1280, 128:256] = jnp.zeros((256, 128), BF)
    dh[384:448, 768:1024] = jnp.zeros((64, 256), BF)
    dl[384:448, 768:1024] = jnp.zeros((64, 256), BF)
    p1[:, GROUPS, :, :] = jnp.zeros((8, 8, 128), F32)
    carry[...] = jnp.zeros((2, 64, 128), F32)

    load_cot.wait()
    for name in ("halves", "pairs", "evens"):
        loads[name].wait()

    def pack(m, _):
        wide = []
        for g in range(4):
            block = cot[16 * g : 16 * g + 16, pl.ds(16 * m, 16), :].reshape(256, 64)
            wide.append(dot(block, k["halves"][...]).astype(BF))
        for g in range(4):
            both = jnp.concatenate([wide[g][:, :128], wide[g][:, 128:]], axis=0)
            two = dot(k["pairs"][...], both).astype(BF)
            cs[pl.ds(8 * m + 1, 8), 16 * g : 16 * g + 16, :] = two.reshape(8, 16, 128)
        for g in range(2):
            both = jnp.concatenate([wide[g][:, :128], wide[g + 2][:, 128:]], axis=0)
            two = dot(k["evens"][...], both).astype(BF)
            cs[pl.ds(8 * m, 8), 64 + 16 * g : 80 + 16 * g, :] = two.reshape(8, 16, 128)
        return 0

    lax.fori_loop(0, 4, pack, 0)

    pl.semaphore_wait(barrier, 41)

    def cot_copy(to, slot):
        return pltpu.make_async_remote_copy(
            src_ref=cs.at[to + 1], dst_ref=cr.at[slot],
            send_sem=cot_send.at[to], recv_sem=cot_recv.at[slot],
            device_id=(mv, to), device_id_type=MESH)

    def send_cot(i, _):
        cot_copy((mg + i) % SLABS, mg).start()
        return 0

    lax.fori_loop(1, SLABS, send_cot, 0)
    cr[mg] = cs[mg + 1]

    load_w.wait()
    wa[...] = jnp.zeros((128, 640), F32)
    for b in range(3):
        for i in range(0, 10, 2):
            (a, e), rows = BACK[i], slice(32 * b, 32 * b + 32)
            first = w[a, b, e].astype(F32)
            if i + 1 < 9:
                a, e = BACK[i + 1]
                second = w[a, b, e].astype(F32)
            else:
                second = jnp.zeros((32, 64), F32)
            wa[rows, 64 * i : 64 * i + 128] = jnp.concatenate([first, second], axis=1)
    for name in ("place", "place_t"):
        loads[name].wait()
    taps = wa[...]
    back = taps.astype(BF)
    front = jnp.transpose(taps).astype(BF)
    for ql in range(5):
        t = dot(k["place"][256 * ql : 256 * ql + 256, :], back).astype(BF)
        tt_oo[:, 256 * ql : 256 * ql + 256] = t[:, 0:256]
        tt_oe[:, 128 * ql : 128 * ql + 128] = t[:, 256:384]
        tt_e[0:256, 128 * ql : 128 * ql + 128] = t[:, 384:512]
        tt_e[256:512, 128 * ql : 128 * ql + 128] = t[:, 512:640]
        t = dot(front, k["place_t"][:, 256 * ql : 256 * ql + 256]).astype(BF)
        for i, pair in enumerate(FRONT):
            j = BACK.index(pair)
            tc[64 * ql : 64 * ql + 64, 256 * i : 256 * i + 256] = t[64 * j : 64 * j + 64, :]

    load_vol.wait()
    loads["spread"].wait()

    def split_x(n, _):
        for parity in range(2):
            both = jnp.concatenate(
                [vol[:, 2 * zz + parity, pl.ds(16 * n, 16), :].reshape(512, 128) for zz in range(2)],
                axis=1)
            s = dot(both, k["spread"][...]).reshape(CI, 16, 384)
            for h in range(2):
                part = s[:, 8 * h : 8 * h + 8, :].reshape(256, 384).astype(BF)
                for e in range(3):
                    row = (3 * parity + e) * 256
                    vc[n, row : row + 256, 128 * h : 128 * h + 128] = part[:, 128 * e : 128 * e + 128]
        return 0

    lax.fori_loop(0, BANDS, split_x, 0)

    lane = lax.broadcasted_iota(jnp.int32, (256, 128), 1)

    def ft_copy(to, slot):
        return pltpu.make_async_remote_copy(
            src_ref=fs.at[to], dst_ref=rf.at[slot + 1],
            send_sem=ft_send.at[to], recv_sem=ft_recv.at[slot],
            device_id=(mv, to), device_id_type=MESH)

    def forward(n, _):
        f01 = dot(tc[:, :1536], vc[n])
        f12 = dot(tc[:, 1536:], vc[n, 768:1536, :])
        for h in range(2):
            a, b = f01[:, 128 * h : 128 * h + 128], f12[:, 128 * h : 128 * h + 128]
            own = jnp.concatenate([a[0:64] + carry[0], a[64:256]], axis=0)
            late = jnp.concatenate([b[0:64] + carry[1], b[64:256]], axis=0)
            carry[0], carry[1] = a[256:320], b[256:320]
            swapped = pltpu.roll(late, 64, 1)
            total = (own + jnp.where(lane >= 64, swapped, 0.0)).astype(BF)
            for ql in range(4):
                q = 8 * n + 4 * h + ql
                low, high = swapped[64 * ql : 64 * ql + 32], late[64 * ql + 32 : 64 * ql + 64]
                fs[q, 0:64, :] = total[64 * ql : 64 * ql + 64]
                fs[q, 64:96, :] = jnp.where(lane[0:32] < 64, low, high).astype(BF)
        return 0

    lax.fori_loop(0, BANDS, forward, 0)

    def send_ft(i, _):
        ft_copy((mg + i) % SLABS, mg).start()
        return 0

    lax.fori_loop(1, SLABS, send_ft, 0)
    rf[mg + 1] = fs[mg]

    def wait_cot(i, _):
        cot_copy((mg + i) % SLABS, (mg + i) % SLABS).wait_recv()
        return 0

    lax.fori_loop(1, SLABS, wait_cot, 0)
    loads["later_lo"].wait()
    loads["later_hi"].wait()

    def forms(n, _):
        blocks = [cr[8 * n + i] for i in range(8)]
        for part, name in ((0, "later_lo"), (1, "later_hi")):
            rows = jnp.concatenate(
                [jnp.concatenate([x_[32 * part : 32 * part + 32], x_[64:96]], axis=1) for x_ in blocks],
                axis=0)
            made = dot(rows, k[name][...]).astype(BF)
            for i in range(8):
                h, ql = i // 4, i % 4
                new = made[32 * i : 32 * i + 32]
                four = (new[:, 0:128], new[:, 128:256], blocks[i][32 * part : 32 * part + 32], new[:, 256:384])
                for v, value in enumerate(four):
                    row = 64 * v + 32 * part
                    c4[n + 1, 256 * ql + row : 256 * ql + row + 32, 128 * h : 128 * h + 128] = value
                    if ql == 0:
                        row += 1024
                        c4[n + h, row : row + 32, 128 * (1 - h) : 128 * (2 - h)] = value
        return 0

    lax.fori_loop(0, BANDS, forms, 0)

    yl = lax.broadcasted_iota(jnp.int32, (64, 256), 1) % 8
    for e in range(3):
        g_odd, g_even = None, None
        for n in range(BANDS):
            later = jnp.concatenate(
                [c4[n + 1, 256 * ql + 64 : 256 * ql + 192, :] for ql in range(5)], axis=0)
            own = jnp.concatenate(
                [c4[n + 1, 256 * ql + 128 : 256 * ql + 192, :] for ql in range(5)], axis=0)
            odd = dot_nt(later, vc[n, 256 * (3 + e) : 256 * (4 + e), :])
            even = dot_nt(own, vc[n, 256 * e : 256 * (e + 1), :])
            g_odd = odd if g_odd is None else g_odd + odd
            g_even = even if g_even is None else g_even + even
        for i in range(3):
            if i == 0:
                g = [g_even[64 * ql : 64 * ql + 64] for ql in range(5)]
            else:
                start = 64 if i == 1 else 0
                g = [g_odd[128 * ql + start : 128 * ql + start + 64] for ql in range(5)]
            d0 = jnp.where(yl == 1, g[1], jnp.where(yl == 3, g[2], jnp.where(
                yl == 5, g[3], jnp.where(yl == 7, g[4], 0.0))))
            rest = jnp.where(yl < 2, g[0], jnp.where(yl < 4, g[1], jnp.where(yl < 6, g[2], g[3])))
            d1, d2 = jnp.where(yl % 2 == 0, rest, 0.0), jnp.where(yl % 2 == 1, rest, 0.0)
            for b, d in enumerate((d0, d1, d2)):
                group, slot = divmod(9 * e + 3 * i + b, 4)
                at = (slice(64 * group, 64 * group + 64), slice(256 * slot, 256 * slot + 256))
                top = d.astype(BF)
                dh[at] = top
                dl[at] = (d - top.astype(F32)).astype(BF)
    loads["bands"].wait()
    packed = dot(dh[...], k["bands"][...]) + dot(dl[...], k["bands"][...])
    for g in range(GROUPS):
        for m in range(8):
            p1[m, g] = packed[64 * g + 8 * m : 64 * g + 8 * m + 8]

    def a_copy(source, target, send, recv, to, slot):
        return pltpu.make_async_remote_copy(
            src_ref=source, dst_ref=target.at[slot], send_sem=send.at[to], recv_sem=recv.at[slot],
            device_id=(z_lo * 4 + to // 2, mg - core + to % 2), device_id_type=MESH)

    def z_copy(source, target, send, recv, to, slot):
        return pltpu.make_async_remote_copy(
            src_ref=source, dst_ref=target.at[slot], send_sem=send.at[to], recv_sem=recv.at[slot],
            device_id=(to % 2 * 4 + y, x * 8 + to // 2 * 2 + core), device_id_type=MESH)

    def x_copy(to, slot):
        return pltpu.make_async_remote_copy(
            src_ref=s2, dst_ref=r3.at[slot], send_sem=x_send.at[to], recv_sem=x_recv.at[slot],
            device_id=(mv, to * 8 + z_hi * 2 + core), device_id_type=MESH)

    loads["weave"].wait()

    def backward(n):
        c = [c4[n + 1, 256 * ql : 256 * ql + 256, :] for ql in range(5)]
        oo = dot(tt_oo[...], c4[n + 1])
        oe = dot(tt_oe[...], jnp.concatenate([v[64:192] for v in c], axis=0))
        ev = dot(tt_e[...], jnp.concatenate([v[128:256] for v in c], axis=0))
        for parity, (at_even, at_odd) in enumerate(((ev[256:512], ev[0:256]), (oe, oo))):
            even, odd = at_even.astype(BF), at_odd.astype(BF)
            parts = []
            for h in range(2):
                lanes = slice(128 * h, 128 * h + 128)
                both = jnp.concatenate([even[:, lanes], odd[:, lanes]], axis=1)
                parts.append(dot(both, k["weave"][...]).reshape(CI, 8, 256))
            out = jnp.concatenate(parts, axis=1).astype(BF)
            for zz in range(2):
                vgrad[:, 2 * zz + parity, 16 * n : 16 * n + 16, :] = out[:, :, 128 * zz : 128 * zz + 128]

    def each(count, me, act):
        for i in range(1, count):
            act((me + i) % count)

    each(8, mine, lambda to: a_copy(p1.at[to], r1, a_send, a_recv, to, mine).start())
    r1[mine] = p1[mine]
    backward(0)
    each(8, mine, lambda to: a_copy(p1.at[to], r1, a_send, a_recv, to, to).wait_recv())
    s1[...] = functools.reduce(jnp.add, [r1[i] for i in range(8)])

    each(8, z, lambda to: z_copy(s1.at[to], r2, z_send, z_recv, to, z).start())
    r2[z] = s1[z]
    backward(1)
    each(8, z, lambda to: z_copy(s1.at[to], r2, z_send, z_recv, to, to).wait_recv())
    s2[...] = functools.reduce(jnp.add, [r2[i] for i in range(8)])

    each(4, x, lambda to: x_copy(to, x).start())
    r3[x] = s2[...]
    backward(2)
    each(4, x, lambda to: x_copy(to, to).wait_recv())
    s3[...] = functools.reduce(jnp.add, [r3[i] for i in range(4)]) * 0.125

    each(8, z, lambda to: z_copy(s3, r4, zz_send, zz_recv, to, z).start())
    r4[z] = s3[...]
    backward(3)
    store_vgrad = pltpu.make_async_copy(vgrad, vgrad_out, out_sem.at[0])
    store_vgrad.start()
    each(8, z, lambda to: z_copy(s3, r4, zz_send, zz_recv, to, to).wait_recv())

    each(8, mine, lambda to: a_copy(r4, r5, aa_send, aa_recv, to, mine).start())
    r5[mine] = r4[...]

    def wait_ft(i, _):
        ft_copy((mg + i) % SLABS, (mg + i) % SLABS).wait_recv()
        return 0

    lax.fori_loop(1, SLABS, wait_ft, 0)
    for name in ("join_lo", "join_hi", "unpick"):
        loads[name].wait()

    def unpack(m, _):
        for g in range(4):
            two = rf[pl.ds(8 * m + 1, 8), 16 * g : 16 * g + 16, :].reshape(128, 128)
            row = 64 + 16 * (g % 2)
            one = rf[pl.ds(8 * m, 8), row : row + 16, :].reshape(128, 128)
            summed = k["join_hi"] if g >= 2 else k["join_lo"]
            planes = dot(jnp.concatenate([two, one], axis=1), summed[...]).astype(BF)
            planes = jnp.concatenate([planes[:, 0:128], planes[:, 128:256]], axis=0)
            rows = dot(k["unpick"][...], planes)[:, 0:64].astype(BF)
            feat[16 * g : 16 * g + 16, pl.ds(16 * m, 16), :] = rows.reshape(16, 16, 64)
        return 0

    lax.fori_loop(0, 4, unpack, 0)
    store_feat = pltpu.make_async_copy(feat, feat_out, out_sem.at[1])
    store_feat.start()

    each(8, mine, lambda to: a_copy(r4, r5, aa_send, aa_recv, to, to).wait_recv())
    for g in range(GROUPS):
        total = jnp.transpose(r5[:, g].reshape(64, 128))
        for slot in range(4):
            if 4 * g + slot < len(TAPS):
                kgrad[TAPS[4 * g + slot]] = total[32 * slot : 32 * slot + 32]
    store_kgrad = pltpu.make_async_copy(kgrad, kgrad_out, out_sem.at[2])
    store_kgrad.start()

    def sent(i, _):
        to = (mg + i) % SLABS
        cot_copy(to, mg).wait_send()
        ft_copy(to, mg).wait_send()
        return 0

    lax.fori_loop(1, SLABS, sent, 0)
    each(8, mine, lambda to: a_copy(p1.at[to], r1, a_send, a_recv, to, mine).wait_send())
    each(8, z, lambda to: z_copy(s1.at[to], r2, z_send, z_recv, to, z).wait_send())
    each(4, x, lambda to: x_copy(to, x).wait_send())
    each(8, z, lambda to: z_copy(s3, r4, zz_send, zz_recv, to, z).wait_send())
    each(8, mine, lambda to: a_copy(r4, r5, aa_send, aa_recv, to, mine).wait_send())
    store_vgrad.wait()
    store_feat.wait()
    store_kgrad.wait()


def shards(volume, weights, cotangent):
    dma = pltpu.SemaphoreType.DMA
    outs = (
        jax.ShapeDtypeStruct((CO, 64, 64), BF),
        jax.ShapeDtypeStruct((CI, 4, 64, 128), BF),
        jax.ShapeDtypeStruct((3, 3, 3, CI, CO), F32),
    )
    scratch = [pltpu.VMEM(value.shape, BF) for _, value in CONSTANTS] + [
        pltpu.VMEM((CI, 4, 64, 128), BF),
        pltpu.VMEM((3, 3, 3, CI, CO), BF),
        pltpu.VMEM((CO, 64, 64), BF),
        pltpu.VMEM((CO, 64, 64), BF),
        pltpu.VMEM((CI, 4, 64, 128), BF),
        pltpu.VMEM((3, 3, 3, CI, CO), F32),
        pltpu.VMEM((SLABS + 1, 96, 128), BF),
        pltpu.VMEM((SLABS, 96, 128), BF),
        pltpu.VMEM((SLABS, 96, 128), BF),
        pltpu.VMEM((SLABS + 1, 96, 128), BF),
        pltpu.VMEM((128, 640), F32),
        pltpu.VMEM((QB, 9 * 256), BF),
        pltpu.VMEM((256, 1280), BF),
        pltpu.VMEM((256, 640), BF),
        pltpu.VMEM((512, 640), BF),
        pltpu.VMEM((BANDS, 1536, 256), BF),
        pltpu.VMEM((BANDS + 1, 1280, 256), BF),
        pltpu.VMEM((2, 64, 128), F32),
        pltpu.VMEM((64 * GROUPS, 1024), BF),
        pltpu.VMEM((64 * GROUPS, 1024), BF),
        pltpu.VMEM((8, 8, 8, 128), F32),
        pltpu.VMEM((8, 8, 8, 128), F32),
        pltpu.VMEM((8, 8, 128), F32),
        pltpu.VMEM((8, 8, 128), F32),
        pltpu.VMEM((8, 128), F32),
        pltpu.VMEM((4, 8, 128), F32),
        pltpu.VMEM((8, 128), F32),
        pltpu.VMEM((8, 8, 128), F32),
        pltpu.VMEM((8, 8, 8, 128), F32),
        dma((3,)), dma((NC,)), dma((3,)),
        dma((SLABS,)), dma((SLABS,)), dma((SLABS,)), dma((SLABS,)),
        dma((8,)), dma((8,)), dma((8,)), dma((8,)), dma((4,)), dma((4,)),
        dma((8,)), dma((8,)), dma((8,)), dma((8,)),
    ]
    anywhere = pl.BlockSpec(memory_space=pl.ANY)
    features, volume_grad, kernel_grad = pl.pallas_call(
        kernel,
        out_shape=outs,
        in_specs=[anywhere] * (3 + NC),
        out_specs=(anywhere,) * 3,
        scratch_shapes=scratch,
        compiler_params=pltpu.CompilerParams(
            collective_id=0, has_side_effects=True, vmem_limit_bytes=56 << 20),
        cost_estimate=pl.CostEstimate(
            flops=2 * 10**10, bytes_accessed=8 << 20, transcendentals=0),
    )(
        volume[0],
        jnp.transpose(weights, (2, 3, 4, 1, 0)),
        cotangent[0, :, :, 0, :],
        *[jnp.asarray(value) for _, value in CONSTANTS],
    )
    return (
        features[None, :, :, None, :],
        volume_grad[None],
        jnp.transpose(kernel_grad, (4, 3, 0, 1, 2)),
    )


def solution(mesh):
    placed = (P("vol", None, "gz", None, None), P(), P("vol", None, None, "gz", None))
    return jax.shard_map(
        shards,
        mesh=mesh,
        in_specs=placed,
        out_specs=(P("vol", None, None, "gz", None), P("vol", None, "gz", None, None), P()),
        check_vma=False,
    )
```

```python
import functools

import jax
import jax.numpy as jnp
import numpy as np
from jax import lax
from jax.experimental import pallas as pl
from jax.experimental.pallas import tpu as pltpu
from jax.sharding import PartitionSpec as P

MESH = pl.DeviceIdType.MESH
BF = jnp.bfloat16
F32 = jnp.float32

CI, CO, SLABS, BANDS = 32, 64, 32, 4
QB = 5 * CO

BACK = ((0, 0), (0, 2), (2, 2), (2, 0), (0, 1), (2, 1), (1, 2), (1, 0), (1, 1))
FRONT = ((1, 0), (1, 1), (1, 2), (2, 0), (2, 1), (2, 2), (0, 0), (0, 1), (0, 2))
TAPS = tuple((a, b, e) for e in range(3) for a in (1, 2, 0) for b in range(3))
GROUPS = 7


def one_hot(rows, columns, test):
    row, column = np.meshgrid(np.arange(rows), np.arange(columns), indexing="ij")
    return np.asarray(test(row, column), np.float32).astype(jnp.bfloat16)


def pair_pick(row, column):
    half, o, p = column // 256, column // 16 % 16, column % 16
    return (row % 16 == o) & (p == 2 * (row // 16) + half)


def even_pick(row, column):
    o, p = column // 16 % 16, column % 16
    return (row % 16 == o) & (p == 2 * (row // 16))


def unpick(row, column):
    half, slab, o = column // 128, column // 16 % 8, column % 16
    return (row // 16 == o) & (row % 16 == 2 * slab + half)


def place(row, column):
    ql, c, yl = row // 256, row // 8 % 32, row % 8
    b, channel = column // 32, column % 32
    return (b < 3) & (c == channel) & (yl == 2 * ql + b - 1)


def spread_x(row, column):
    zz, x = row // 128, row % 128
    e, half, r = column // 128, column // 64 % 2, column % 64
    return (zz == half) & (x == 2 * r + e - 1)


def weave_x(row, column):
    parity, zz, r = row // 128, row // 64 % 2, row % 64
    return (zz == column // 128) & (column % 128 == 2 * r + parity)


def shift_left(row, column):
    return (column % 64 < 63) & (row == column + 1)


def later_planes(high, row, column):
    shift = 1 - column // 128
    lane = column % 128 + shift
    valid = (column % 64 + shift) < 64
    return valid & (row == np.where(lane < 64, lane + 64, 128 + lane - (0 if high else 64)))


def squeeze(row, column):
    return (row // 128 == column // 64) & (row % 128 == column % 64)


def halves(row, column):
    return (column % 64 == row) & ((column // 64 == 0) | (column // 64 == 3))


def join(upper, row, column):
    even = (row == column) | (row == 128 + 64 * upper + column)
    odd = row == column - 64
    return np.where(column < 64, even, (column // 64 == 2) & odd)


def sum_band(row, column):
    return row // 8 == column


CONSTANTS = (
    ("halves", one_hot(64, 256, halves)),
    ("pairs", one_hot(128, 512, pair_pick)),
    ("evens", one_hot(128, 512, even_pick)),
    ("place", one_hot(5 * 256, 128, place)),
    ("place_t", np.ascontiguousarray(one_hot(5 * 256, 128, place).T)),
    ("spread", one_hot(256, 384, spread_x)),
    ("squeeze", one_hot(256, 128, squeeze)),
    ("shift", one_hot(128, 128, shift_left)),
    ("later_lo", one_hot(256, 256, functools.partial(later_planes, False))),
    ("later_hi", one_hot(256, 256, functools.partial(later_planes, True))),
    ("bands", one_hot(1024, 128, sum_band)),
    ("weave", one_hot(256, 256, weave_x)),
    ("join_lo", one_hot(256, 256, functools.partial(join, 0))),
    ("join_hi", one_hot(256, 256, functools.partial(join, 1))),
    ("unpick", one_hot(256, 256, unpick)),
)
NC = len(CONSTANTS)


def dot(a, b):
    return jnp.dot(a, b, preferred_element_type=F32)


def dot_nt(a, b):
    return lax.dot_general(a, b, (((1,), (1,)), ((), ())), preferred_element_type=F32)


def kernel(*refs):
    (vol_in, w_in, cot_in), refs = refs[:3], refs[3:]
    const_in, refs = refs[:NC], refs[NC:]
    (feat, vgrad, gathered), refs = refs[:3], refs[3:]
    const, refs = refs[:NC], refs[NC:]
    k = {name: ref for (name, _), ref in zip(CONSTANTS, const)}
    (vol, w, cot, cs, cr, near, fw, late_in, fs, rf, wa, tc, tt_oo, tt_oe, tt_e, vc, c4, carry,
     dh, dl, terms, part_in, part, whole_in, whole,
     in_sem, const_sem, cot_send, cot_recv, near_send, near_recv, late_send, late_recv,
     ft_send, ft_recv, part_send, part_recv, whole_send, whole_recv, last_send, last_recv) = refs

    mv, mg = lax.axis_index("vol"), lax.axis_index("gz")
    y, z_lo = mv % 4, mv // 4
    core, z_hi, x = mg % 2, mg // 2 % 4, mg // 8
    mine, z = x * 8 + y * 2 + core, z_hi * 2 + z_lo

    barrier = pltpu.get_barrier_semaphore()

    def greet(v, g):
        pl.semaphore_signal(barrier, inc=1, device_id=(v, g), device_id_type=MESH)

    def greet_slab(i, _):
        greet(mv, (mg + i) % SLABS)
        return 0

    lax.fori_loop(1, SLABS, greet_slab, 0)

    def greet_layer(i, _):
        greet(z_lo * 4 + (y + i // 8) % 4, (i % 8 // 2) * 8 + z_hi * 2 + i % 2)
        return 0

    lax.fori_loop(8, 32, greet_layer, 0)
    for other in range(4):
        greet((1 - z_lo) * 4 + y, x * 8 + other * 2 + core)

    load_cot = pltpu.make_async_copy(cot_in, cot, in_sem.at[0])
    load_w = pltpu.make_async_copy(w_in, w, in_sem.at[1])
    load_vol = pltpu.make_async_copy(vol_in, vol, in_sem.at[2])
    loads = {
        name: pltpu.make_async_copy(const_in[i], const[i], const_sem.at[i])
        for i, (name, _) in enumerate(CONSTANTS)
    }
    load_cot.start()
    for name in ("halves", "pairs", "evens"):
        loads[name].start()
    load_w.start()
    load_vol.start()
    for name in list(loads)[3:]:
        loads[name].start()

    cs[SLABS, 64:96, :] = jnp.zeros((32, 128), BF)
    rf[0, 64:96, :] = jnp.zeros((32, 128), BF)
    for slot in range(1, SLABS, 2):
        rf[slot, 64:96, :] = jnp.zeros((32, 128), BF)
    c4[BANDS, 1024:1280, 128:256] = jnp.zeros((256, 128), BF)
    dh[384:448, 768:1024] = jnp.zeros((64, 256), BF)
    dl[384:448, 768:1024] = jnp.zeros((64, 256), BF)
    terms[28:32] = jnp.zeros((4, 16, 128), F32)
    carry[...] = jnp.zeros((2, 64, 128), F32)

    load_cot.wait()
    for name in ("halves", "pairs", "evens"):
        loads[name].wait()

    def pack(m, _):
        wide = []
        for g in range(4):
            block = cot[16 * g : 16 * g + 16, pl.ds(16 * m, 16), :].reshape(256, 64)
            wide.append(dot(block, k["halves"][...]).astype(BF))
        for g in range(4):
            both = jnp.concatenate([wide[g][:, :128], wide[g][:, 128:]], axis=0)
            two = dot(k["pairs"][...], both).astype(BF)
            cs[pl.ds(8 * m + 1, 8), 16 * g : 16 * g + 16, :] = two.reshape(8, 16, 128)
        for g in range(2):
            both = jnp.concatenate([wide[g][:, :128], wide[g + 2][:, 128:]], axis=0)
            two = dot(k["evens"][...], both).astype(BF)
            cs[pl.ds(8 * m, 8), 64 + 16 * g : 80 + 16 * g, :] = two.reshape(8, 16, 128)
        return 0

    lax.fori_loop(0, 4, pack, 0)

    pl.semaphore_wait(barrier, 59)

    def cot_copy(to, rows):
        return pltpu.make_async_remote_copy(
            src_ref=cs.at[to + 1, 0:rows], dst_ref=cr.at[mg, 0:rows],
            send_sem=cot_send.at[0], recv_sem=cot_recv.at[0],
            device_id=(mv, to), device_id_type=MESH)

    cr[mg, 0:64] = cs[mg + 1, 0:64]

    @pl.when(core == 1)
    def _():
        cr[mg, 64:96] = cs[mg + 1, 64:96]

    def send_cot(i, _):
        to = (mg + i) % SLABS

        @pl.when(to % 2 == 0)
        def _():
            cot_copy(to, 64).start()

        @pl.when(to % 2 == 1)
        def _():
            cot_copy(to, 96).start()

        return 0

    lax.fori_loop(1, SLABS, send_cot, 0)

    def arrived(buffer, sem):
        pltpu.make_async_copy(buffer, buffer, sem.at[0]).wait()

    load_w.wait()
    wa[...] = jnp.zeros((128, 640), F32)
    for b in range(3):
        for i in range(0, 10, 2):
            (a, e), rows = BACK[i], slice(32 * b, 32 * b + 32)
            first = w[a, b, e].astype(F32)
            if i + 1 < 9:
                a, e = BACK[i + 1]
                second = w[a, b, e].astype(F32)
            else:
                second = jnp.zeros((32, 64), F32)
            wa[rows, 64 * i : 64 * i + 128] = jnp.concatenate([first, second], axis=1)
    for name in ("place", "place_t"):
        loads[name].wait()
    taps = wa[...]
    back = taps.astype(BF)
    front = jnp.transpose(taps).astype(BF)
    for ql in range(5):
        t = dot(k["place"][256 * ql : 256 * ql + 256, :], back).astype(BF)
        tt_oo[:, 256 * ql : 256 * ql + 256] = t[:, 0:256]
        tt_oe[:, 128 * ql : 128 * ql + 128] = t[:, 256:384]
        tt_e[0:256, 128 * ql : 128 * ql + 128] = t[:, 384:512]
        tt_e[256:512, 128 * ql : 128 * ql + 128] = t[:, 512:640]
        t = dot(front, k["place_t"][:, 256 * ql : 256 * ql + 256]).astype(BF)
        for i, pair in enumerate(FRONT):
            j = BACK.index(pair)
            tc[64 * ql : 64 * ql + 64, 256 * i : 256 * i + 256] = t[64 * j : 64 * j + 64, :]

    load_vol.wait()
    loads["spread"].wait()

    def split_x(n, _):
        for parity in range(2):
            both = jnp.concatenate(
                [vol[:, 2 * zz + parity, pl.ds(16 * n, 16), :].reshape(512, 128) for zz in range(2)],
                axis=1)
            s = dot(both, k["spread"][...]).reshape(CI, 16, 384)
            for h in range(2):
                part = s[:, 8 * h : 8 * h + 8, :].reshape(256, 384).astype(BF)
                for e in range(3):
                    row = (3 * parity + e) * 256
                    vc[n, row : row + 256, 128 * h : 128 * h + 128] = part[:, 128 * e : 128 * e + 128]
        return 0

    lax.fori_loop(0, BANDS, split_x, 0)

    lane = lax.broadcasted_iota(jnp.int32, (256, 128), 1)

    def ft_copy(to, rows):
        return pltpu.make_async_remote_copy(
            src_ref=fs.at[to, 0:rows], dst_ref=rf.at[mg + 1, 0:rows],
            send_sem=ft_send.at[0], recv_sem=ft_recv.at[0],
            device_id=(mv, to), device_id_type=MESH)

    def forward(n, _):
        f01 = dot(tc[:, :1536], vc[n])
        f12 = dot(tc[:, 1536:], vc[n, 768:1536, :])
        for h in range(2):
            a, b = f01[:, 128 * h : 128 * h + 128], f12[:, 128 * h : 128 * h + 128]
            own = jnp.concatenate([a[0:64] + carry[0], a[64:256]], axis=0)
            late = jnp.concatenate([b[0:64] + carry[1], b[64:256]], axis=0)
            carry[0], carry[1] = a[256:320], b[256:320]
            swapped = pltpu.roll(late, 64, 1)
            total = own + jnp.where(lane >= 64, swapped, 0.0)
            for ql in range(4):
                q = 8 * n + 4 * h + ql
                low, high = swapped[64 * ql : 64 * ql + 32], late[64 * ql + 32 : 64 * ql + 64]
                fw[q] = total[64 * ql : 64 * ql + 64]
                fs[q, 64:96, :] = jnp.where(lane[0:32] < 64, low, high).astype(BF)
        return 0

    lax.fori_loop(0, BANDS, forward, 0)

    late_copy = pltpu.make_async_remote_copy(
        src_ref=fs.at[:, 64:96], dst_ref=late_in, send_sem=late_send.at[0], recv_sem=late_recv.at[0],
        device_id=(mv, mg + 1 - 2 * core), device_id_type=MESH)

    @pl.when(core == 0)
    def _():
        late_copy.start()

        def round_off(q, _):
            fs[q, 0:64] = fw[q].astype(BF)
            return 0

        lax.fori_loop(0, SLABS, round_off, 0)
        rf[mg + 1, 0:64] = fs[mg, 0:64]

    @pl.when(core == 1)
    def _():
        late_copy.wait_recv()

        def add_late(q, _):
            both = late_in[q].astype(F32)
            both = jnp.concatenate([both, pltpu.roll(both, 64, 1)], axis=0)
            fs[q, 0:64] = (fw[q] + jnp.where(lane[0:64] < 64, both, 0.0)).astype(BF)
            return 0

        lax.fori_loop(0, SLABS, add_late, 0)
        rf[mg + 1] = fs[mg]

    def send_ft(i, _):
        to = (mg + i) % SLABS

        @pl.when(core == 0)
        def _():
            ft_copy(to, 64).start()

        @pl.when(core == 1)
        def _():
            ft_copy(to, 96).start()

        return 0

    @pl.when(core == 0)
    def _():
        arrived(cr.at[0:31, 0:64], cot_recv)

    @pl.when(core == 1)
    def _():
        arrived(cr.at[0:31, 0:96], cot_recv)

    near_copy = pltpu.make_async_remote_copy(
        src_ref=near, dst_ref=cr.at[:, 64:96], send_sem=near_send.at[0], recv_sem=near_recv.at[0],
        device_id=(mv, mg + 1 - 2 * core), device_id_type=MESH)
    for name in ("squeeze", "shift", "later_lo", "later_hi"):
        loads[name].wait()

    @pl.when(core == 1)
    def _():
        def pass_on(n, _):
            rows = jnp.concatenate(
                [jnp.concatenate([cr[8 * n + i, 0:32], cr[8 * n + i, 32:64]], axis=1) for i in range(8)],
                axis=0)
            near[pl.ds(8 * n, 8)] = dot(rows, k["squeeze"][...]).astype(BF).reshape(8, 32, 128)
            return 0

        lax.fori_loop(0, BANDS, pass_on, 0)
        near_copy.start()

    lax.fori_loop(1, SLABS, send_ft, 0)

    def keep(n, h, ql, row, value):
        size = value.shape[0]
        c4[n + 1, 256 * ql + row : 256 * ql + row + size, 128 * h : 128 * h + 128] = value
        if ql == 0:
            c4[n + h, 1024 + row : 1024 + row + size, 128 * (1 - h) : 128 * (2 - h)] = value

    def forms_own(n, _):
        blocks = [cr[8 * n + i, 0:64] for i in range(8)]
        moved = dot(jnp.concatenate(blocks, axis=0), k["shift"][...]).astype(BF)
        for i in range(8):
            keep(n, i // 4, i % 4, 128, blocks[i])
            keep(n, i // 4, i % 4, 192, moved[64 * i : 64 * i + 64])
        return 0

    lax.fori_loop(0, BANDS, forms_own, 0)

    def forms_later(n, _):
        blocks = [cr[8 * n + i] for i in range(8)]
        for part_, name in ((0, "later_lo"), (1, "later_hi")):
            rows = jnp.concatenate(
                [jnp.concatenate([v[32 * part_ : 32 * part_ + 32], v[64:96]], axis=1) for v in blocks],
                axis=0)
            made = dot(rows, k[name][...]).astype(BF)
            for i in range(8):
                new = made[32 * i : 32 * i + 32]
                keep(n, i // 4, i % 4, 32 * part_, new[:, 0:128])
                keep(n, i // 4, i % 4, 64 + 32 * part_, new[:, 128:256])
        return 0

    yl = lax.broadcasted_iota(jnp.int32, (64, 256), 1) % 8

    def gradient(i, e):
        total = None
        start, taps = (64 if i == 2 else 128), 256 * (e + (0 if i == 0 else 3))
        for n in range(BANDS):
            rows = jnp.concatenate(
                [c4[n + 1, 256 * ql + start : 256 * ql + start + 64, :] for ql in range(5)], axis=0)
            term = dot_nt(rows, vc[n, taps : taps + 256, :])
            total = term if total is None else total + term
        g = [total[64 * ql : 64 * ql + 64] for ql in range(5)]
        d0 = jnp.where(yl == 1, g[1], jnp.where(yl == 3, g[2], jnp.where(
            yl == 5, g[3], jnp.where(yl == 7, g[4], 0.0))))
        rest = jnp.where(yl < 2, g[0], jnp.where(yl < 4, g[1], jnp.where(yl < 6, g[2], g[3])))
        d1, d2 = jnp.where(yl % 2 == 0, rest, 0.0), jnp.where(yl % 2 == 1, rest, 0.0)
        for b, d in enumerate((d0, d1, d2)):
            group, slot = divmod(9 * e + 3 * i + b, 4)
            at = (slice(64 * group, 64 * group + 64), slice(256 * slot, 256 * slot + 256))
            top = d.astype(BF)
            dh[at] = top
            dl[at] = (d - top.astype(F32)).astype(BF)

    for e in range(3):
        gradient(0, e)
        gradient(1, e)

    @pl.when(core == 0)
    def _():
        near_copy.wait_recv()

    lax.fori_loop(0, BANDS, forms_later, 0)
    for e in range(3):
        gradient(2, e)
    loads["bands"].wait()
    packed = dot(dh[...], k["bands"][...]) + dot(dl[...], k["bands"][...])
    terms[0:28] = packed.reshape(28, 16, 128)

    def layer_copy(source, target, send, recv, to, slot):
        return pltpu.make_async_remote_copy(
            src_ref=source, dst_ref=target.at[slot], send_sem=send.at[0], recv_sem=recv.at[0],
            device_id=(z_lo * 4 + to // 2 % 4, to // 8 * 8 + z_hi * 2 + to % 2), device_id_type=MESH)

    def part_copy(to, slot):
        return layer_copy(terms.at[to], part_in, part_send, part_recv, to, slot)

    def last_copy(to, slot):
        return layer_copy(whole, gathered, last_send, last_recv, to, slot)

    def whole_copy(to, slot):
        return pltpu.make_async_remote_copy(
            src_ref=part, dst_ref=whole_in.at[slot],
            send_sem=whole_send.at[0], recv_sem=whole_recv.at[0],
            device_id=(to % 2 * 4 + y, x * 8 + to // 2 * 2 + core), device_id_type=MESH)

    loads["weave"].wait()

    def backward(n):
        c = [c4[n + 1, 256 * ql : 256 * ql + 256, :] for ql in range(5)]
        oo = dot(tt_oo[...], c4[n + 1])
        oe = dot(tt_oe[...], jnp.concatenate([v[64:192] for v in c], axis=0))
        ev = dot(tt_e[...], jnp.concatenate([v[128:256] for v in c], axis=0))
        for parity, (at_even, at_odd) in enumerate(((ev[256:512], ev[0:256]), (oe, oo))):
            even, odd = at_even.astype(BF), at_odd.astype(BF)
            parts = []
            for h in range(2):
                lanes = slice(128 * h, 128 * h + 128)
                both = jnp.concatenate([even[:, lanes], odd[:, lanes]], axis=1)
                parts.append(dot(both, k["weave"][...]).reshape(CI, 8, 256))
            out = jnp.concatenate(parts, axis=1).astype(BF)
            for zz in range(2):
                vgrad[:, 2 * zz + parity, 16 * n : 16 * n + 16, :] = out[:, :, 128 * zz : 128 * zz + 128]

    def each(count, me, act):
        def step(i, _):
            act((me + i) % count)
            return 0

        lax.fori_loop(1, count, step, 0)

    each(32, mine, lambda to: part_copy(to, mine).start())
    part_in[mine] = terms[mine]

    @pl.when(core == 0)
    def _():
        late_copy.wait_send()
        arrived(vc.at[0, 0:1248], cot_send)

    @pl.when(core == 1)
    def _():
        near_copy.wait_send()
        arrived(vc.at[0, 0:1232], cot_send)

    backward(0)
    arrived(part_in.at[0:31], part_recv)
    part[...] = functools.reduce(jnp.add, [part_in[i] for i in range(32)])

    each(8, z, lambda to: whole_copy(to, z).start())
    whole_in[z] = part[...]
    arrived(terms.at[0:31], part_send)
    backward(1)
    arrived(whole_in.at[0:7], whole_recv)
    whole[...] = (functools.reduce(jnp.add, [whole_in[i] for i in range(8)]) * 0.125).astype(BF)

    each(32, mine, lambda to: last_copy(to, mine).start())
    gathered[mine] = whole[...]
    arrived(whole_in.at[0:7], whole_send)
    backward(2)
    backward(3)

    @pl.when(core == 0)
    def _():
        arrived(vc.at[0, 0:1248], ft_recv)
        arrived(fs.at[0:31, 0:64], ft_send)

    @pl.when(core == 1)
    def _():
        arrived(vc.at[0, 0:1232], ft_recv)
        arrived(fs.at[0:31, 0:96], ft_send)

    for name in ("join_lo", "join_hi", "unpick"):
        loads[name].wait()

    def unpack(m, _):
        for g in range(4):
            two = rf[pl.ds(8 * m + 1, 8), 16 * g : 16 * g + 16, :].reshape(128, 128)
            row = 64 + 16 * (g % 2)
            one = rf[pl.ds(8 * m, 8), row : row + 16, :].reshape(128, 128)
            summed = k["join_hi"] if g >= 2 else k["join_lo"]
            planes = dot(jnp.concatenate([two, one], axis=1), summed[...]).astype(BF)
            planes = jnp.concatenate([planes[:, 0:128], planes[:, 128:256]], axis=0)
            rows = dot(k["unpick"][...], planes)[:, 0:64].astype(BF)
            feat[16 * g : 16 * g + 16, pl.ds(16 * m, 16), :] = rows.reshape(16, 16, 64)
        return 0

    lax.fori_loop(0, 4, unpack, 0)

    arrived(gathered.at[0:31], last_recv)
    arrived(gathered.at[0:31], last_send)


def store(feat, vgrad, gathered, feat_out, vgrad_out, kgrad_out, kgrad, sem):
    copies = [
        pltpu.make_async_copy(source, target, sem.at[i])
        for i, (source, target) in enumerate(
            ((vgrad, vgrad_out), (feat, feat_out), (kgrad, kgrad_out)))
    ]
    copies[0].start()
    copies[1].start()
    for g in range(GROUPS):
        total = jnp.transpose(gathered[4 * g : 4 * g + 4].astype(F32).reshape(64, 128))
        for slot in range(4):
            if 4 * g + slot < len(TAPS):
                kgrad[TAPS[4 * g + slot]] = total[32 * slot : 32 * slot + 32]
    copies[2].start()
    for copy in copies:
        copy.wait()


def shards(volume, weights, cotangent):
    dma = pltpu.SemaphoreType.DMA
    outs = (
        jax.ShapeDtypeStruct((CO, 64, 64), BF),
        jax.ShapeDtypeStruct((CI, 4, 64, 128), BF),
        jax.ShapeDtypeStruct((3, 3, 3, CI, CO), F32),
    )
    held = (
        pltpu.VMEM((CO, 64, 64), BF),
        pltpu.VMEM((CI, 4, 64, 128), BF),
        pltpu.VMEM((32, 16, 128), BF),
    )
    scratch = [pltpu.VMEM(value.shape, BF) for _, value in CONSTANTS] + [
        pltpu.VMEM((CI, 4, 64, 128), BF),
        pltpu.VMEM((3, 3, 3, CI, CO), BF),
        pltpu.VMEM((CO, 64, 64), BF),
        pltpu.VMEM((SLABS + 1, 96, 128), BF),
        pltpu.VMEM((SLABS, 96, 128), BF),
        pltpu.VMEM((SLABS, 32, 128), BF),
        pltpu.VMEM((SLABS, 64, 128), F32),
        pltpu.VMEM((SLABS, 32, 128), BF),
        pltpu.VMEM((SLABS, 96, 128), BF),
        pltpu.VMEM((SLABS + 1, 96, 128), BF),
        pltpu.VMEM((128, 640), F32),
        pltpu.VMEM((QB, 9 * 256), BF),
        pltpu.VMEM((256, 1280), BF),
        pltpu.VMEM((256, 640), BF),
        pltpu.VMEM((512, 640), BF),
        pltpu.VMEM((BANDS, 1536, 256), BF),
        pltpu.VMEM((BANDS + 1, 1280, 256), BF),
        pltpu.VMEM((2, 64, 128), F32),
        pltpu.VMEM((64 * GROUPS, 1024), BF),
        pltpu.VMEM((64 * GROUPS, 1024), BF),
        pltpu.VMEM((32, 16, 128), F32),
        pltpu.VMEM((32, 16, 128), F32),
        pltpu.VMEM((16, 128), F32),
        pltpu.VMEM((8, 16, 128), F32),
        pltpu.VMEM((16, 128), BF),
        dma((3,)), dma((NC,)),
        *[dma((1,))] * 14,
    ]
    anywhere = pl.BlockSpec(memory_space=pltpu.HBM)
    inside = pl.BlockSpec(memory_space=pltpu.VMEM)
    results = pl.pallas_call(
        kernel,
        out_shape=held,
        in_specs=[anywhere] * (3 + NC),
        out_specs=(inside,) * 3,
        scratch_shapes=scratch,
        compiler_params=pltpu.CompilerParams(
            collective_id=0, has_side_effects=True, vmem_limit_bytes=40 << 20),
        cost_estimate=pl.CostEstimate(
            flops=2 * 10**10, bytes_accessed=8 << 20, transcendentals=0),
    )(*[
        pltpu.with_memory_space_constraint(value, pltpu.HBM)
        for value in (
            volume[0],
            jnp.transpose(weights, (2, 3, 4, 1, 0)),
            cotangent[0, :, :, 0, :],
            *[jnp.asarray(value) for _, value in CONSTANTS],
        )
    ])
    features, volume_grad, kernel_grad = pl.pallas_call(
        store,
        out_shape=outs,
        in_specs=[inside] * 3,
        out_specs=(anywhere,) * 3,
        scratch_shapes=[pltpu.VMEM((3, 3, 3, CI, CO), F32), dma((3,))],
        compiler_params=pltpu.CompilerParams(vmem_limit_bytes=8 << 20),
    )(*[pltpu.with_memory_space_constraint(value, pltpu.VMEM) for value in results])
    return (
        features[None, :, :, None, :],
        volume_grad[None],
        jnp.transpose(kernel_grad, (4, 3, 0, 1, 2)),
    )


def solution(mesh):
    placed = (P("vol", None, "gz", None, None), P(), P("vol", None, None, "gz", None))
    return jax.shard_map(
        shards,
        mesh=mesh,
        in_specs=placed,
        out_specs=(P("vol", None, None, "gz", None), P("vol", None, "gz", None, None), P()),
        check_vma=False,
    )
```

```python
import functools

import jax
import jax.numpy as jnp
import numpy as np
from jax import lax
from jax.experimental import pallas as pl
from jax.experimental.pallas import tpu as pltpu
from jax.sharding import PartitionSpec as P

MESH = pl.DeviceIdType.MESH
BF = jnp.bfloat16
F32 = jnp.float32

CI, CO, SLABS, BANDS = 32, 64, 32, 4
QB = 5 * CO

BACK = ((0, 0), (0, 2), (2, 2), (2, 0), (0, 1), (2, 1), (1, 2), (1, 0), (1, 1))
FRONT = ((1, 0), (1, 1), (1, 2), (2, 0), (2, 1), (2, 2), (0, 0), (0, 1), (0, 2))
TAPS = tuple((a, b, e) for e in range(3) for a in (1, 2, 0) for b in range(3))
GROUPS = 7


def one_hot(rows, columns, test):
    row, column = np.meshgrid(np.arange(rows), np.arange(columns), indexing="ij")
    return np.asarray(test(row, column), np.float32).astype(jnp.bfloat16)


def pair_pick(row, column):
    half, o, p = column // 256, column // 16 % 16, column % 16
    return (row % 16 == o) & (p == 2 * (row // 16) + half)


def even_pick(row, column):
    o, p = column // 16 % 16, column % 16
    return (row % 16 == o) & (p == 2 * (row // 16))


def unpick(row, column):
    half, slab, o = column // 128, column // 16 % 8, column % 16
    return (row // 16 == o) & (row % 16 == 2 * slab + half)


def place(row, column):
    ql, c, yl = row // 256, row // 8 % 32, row % 8
    b, channel = column // 32, column % 32
    return (b < 3) & (c == channel) & (yl == 2 * ql + b - 1)


def spread_x(row, column):
    zz, x = row // 128, row % 128
    e, half, r = column // 128, column // 64 % 2, column % 64
    return (zz == half) & (x == 2 * r + e - 1)


def weave_x(row, column):
    parity, zz, r = row // 128, row // 64 % 2, row % 64
    return (zz == column // 128) & (column % 128 == 2 * r + parity)


def shift_left(row, column):
    return (column % 64 < 63) & (row == column + 1)


def later_planes(high, row, column):
    shift = 1 - column // 128
    lane = column % 128 + shift
    valid = (column % 64 + shift) < 64
    return valid & (row == np.where(lane < 64, lane + 64, 128 + lane - (0 if high else 64)))


def squeeze(row, column):
    return (row // 128 == column // 64) & (row % 128 == column % 64)


def halves(row, column):
    return (column % 64 == row) & ((column // 64 == 0) | (column // 64 == 3))


def join(upper, row, column):
    even = (row == column) | (row == 128 + 64 * upper + column)
    odd = row == column - 64
    return np.where(column < 64, even, (column // 64 == 2) & odd)


def sum_band(row, column):
    return row // 8 == column


CONSTANTS = (
    ("halves", one_hot(64, 256, halves)),
    ("pairs", one_hot(128, 512, pair_pick)),
    ("evens", one_hot(128, 512, even_pick)),
    ("place", one_hot(5 * 256, 128, place)),
    ("place_t", np.ascontiguousarray(one_hot(5 * 256, 128, place).T)),
    ("spread", one_hot(256, 384, spread_x)),
    ("squeeze", one_hot(256, 128, squeeze)),
    ("shift", one_hot(128, 128, shift_left)),
    ("later_lo", one_hot(256, 256, functools.partial(later_planes, False))),
    ("later_hi", one_hot(256, 256, functools.partial(later_planes, True))),
    ("bands", one_hot(1024, 128, sum_band)),
    ("weave", one_hot(256, 256, weave_x)),
    ("join_lo", one_hot(256, 256, functools.partial(join, 0))),
    ("join_hi", one_hot(256, 256, functools.partial(join, 1))),
    ("unpick", one_hot(256, 256, unpick)),
)
NC = len(CONSTANTS)


def dot(a, b):
    return jnp.dot(a, b, preferred_element_type=F32)


def dot_nt(a, b):
    return lax.dot_general(a, b, (((1,), (1,)), ((), ())), preferred_element_type=F32)


def kernel(*refs):
    (vol_in, w_in, cot_in), refs = refs[:3], refs[3:]
    const_in, refs = refs[:NC], refs[NC:]
    (feat, vgrad, gathered), refs = refs[:3], refs[3:]
    const, refs = refs[:NC], refs[NC:]
    k = {name: ref for (name, _), ref in zip(CONSTANTS, const)}
    (vol, w, cot, cs, cr, near, fw, late_in, fs, rf, wa, tc, tt_oo, tt_oe, tt_e, vc, c4, carry,
     dh, dl, terms, part_in, part, whole_in, whole,
     in_sem, const_sem, cot_send, cot_recv, near_send, near_recv, late_send, late_recv,
     ft_send, ft_recv, part_send, part_recv, whole_send, whole_recv, last_send, last_recv) = refs

    mv, mg = lax.axis_index("vol"), lax.axis_index("gz")
    y, z_lo = mv % 4, mv // 4
    core, z_hi, x = mg % 2, mg // 2 % 4, mg // 8
    mine, z = x * 8 + y * 2 + core, z_hi * 2 + z_lo

    barrier = pltpu.get_barrier_semaphore()

    def greet(v, g):
        pl.semaphore_signal(barrier, inc=1, device_id=(v, g), device_id_type=MESH)

    def greet_slab(i, _):
        greet(mv, (mg + i) % SLABS)
        return 0

    lax.fori_loop(1, SLABS, greet_slab, 0)

    def greet_layer(i, _):
        greet(z_lo * 4 + (y + i // 8) % 4, (i % 8 // 2) * 8 + z_hi * 2 + i % 2)
        return 0

    lax.fori_loop(8, 32, greet_layer, 0)
    for other in range(4):
        greet((1 - z_lo) * 4 + y, x * 8 + other * 2 + core)

    load_cot = pltpu.make_async_copy(cot_in, cot, in_sem.at[0])
    load_w = pltpu.make_async_copy(w_in, w, in_sem.at[1])
    load_vol = pltpu.make_async_copy(vol_in, vol, in_sem.at[2])
    loads = {
        name: pltpu.make_async_copy(const_in[i], const[i], const_sem.at[i])
        for i, (name, _) in enumerate(CONSTANTS)
    }
    load_cot.start()
    for name in ("halves", "pairs", "evens"):
        loads[name].start()
    load_w.start()
    load_vol.start()
    for name in list(loads)[3:]:
        loads[name].start()

    cs[SLABS, 64:96, :] = jnp.zeros((32, 128), BF)
    rf[0, 64:96, :] = jnp.zeros((32, 128), BF)
    for slot in range(1, SLABS, 2):
        rf[slot, 64:96, :] = jnp.zeros((32, 128), BF)
    c4[BANDS, 1024:1280, 128:256] = jnp.zeros((256, 128), BF)
    dh[384:448, 768:1024] = jnp.zeros((64, 256), BF)
    dl[384:448, 768:1024] = jnp.zeros((64, 256), BF)
    terms[28:32] = jnp.zeros((4, 16, 128), F32)
    carry[...] = jnp.zeros((2, 64, 128), F32)

    load_cot.wait()
    for name in ("halves", "pairs", "evens"):
        loads[name].wait()

    def pack(m, _):
        wide = []
        for g in range(4):
            block = cot[16 * g : 16 * g + 16, pl.ds(16 * m, 16), :].reshape(256, 64)
            wide.append(dot(block, k["halves"][...]).astype(BF))
        for g in range(4):
            both = jnp.concatenate([wide[g][:, :128], wide[g][:, 128:]], axis=0)
            two = dot(k["pairs"][...], both).astype(BF)
            cs[pl.ds(8 * m + 1, 8), 16 * g : 16 * g + 16, :] = two.reshape(8, 16, 128)
        for g in range(2):
            both = jnp.concatenate([wide[g][:, :128], wide[g + 2][:, 128:]], axis=0)
            two = dot(k["evens"][...], both).astype(BF)
            cs[pl.ds(8 * m, 8), 64 + 16 * g : 80 + 16 * g, :] = two.reshape(8, 16, 128)
        return 0

    lax.fori_loop(0, 4, pack, 0)

    pl.semaphore_wait(barrier, 59)

    def cot_copy(to, rows):
        return pltpu.make_async_remote_copy(
            src_ref=cs.at[to + 1, 0:rows], dst_ref=cr.at[mg, 0:rows],
            send_sem=cot_send.at[0], recv_sem=cot_recv.at[0],
            device_id=(mv, to), device_id_type=MESH)

    cr[mg, 0:64] = cs[mg + 1, 0:64]

    @pl.when(core == 1)
    def _():
        cr[mg, 64:96] = cs[mg + 1, 64:96]

    def send_cot(i, _):
        to = (mg + 5 * i) % SLABS

        @pl.when(to % 2 == 0)
        def _():
            cot_copy(to, 64).start()

        @pl.when(to % 2 == 1)
        def _():
            cot_copy(to, 96).start()

        return 0

    lax.fori_loop(1, SLABS, send_cot, 0)

    def arrived(buffer, sem):
        pltpu.make_async_copy(buffer, buffer, sem.at[0]).wait()

    load_w.wait()
    wa[...] = jnp.zeros((128, 640), F32)
    for b in range(3):
        for i in range(0, 10, 2):
            (a, e), rows = BACK[i], slice(32 * b, 32 * b + 32)
            first = w[a, b, e].astype(F32)
            if i + 1 < 9:
                a, e = BACK[i + 1]
                second = w[a, b, e].astype(F32)
            else:
                second = jnp.zeros((32, 64), F32)
            wa[rows, 64 * i : 64 * i + 128] = jnp.concatenate([first, second], axis=1)
    for name in ("place", "place_t"):
        loads[name].wait()
    taps = wa[...]
    back = taps.astype(BF)
    front = jnp.transpose(taps).astype(BF)
    for ql in range(5):
        t = dot(k["place"][256 * ql : 256 * ql + 256, :], back).astype(BF)
        tt_oo[:, 256 * ql : 256 * ql + 256] = t[:, 0:256]
        tt_oe[:, 128 * ql : 128 * ql + 128] = t[:, 256:384]
        tt_e[0:256, 128 * ql : 128 * ql + 128] = t[:, 384:512]
        tt_e[256:512, 128 * ql : 128 * ql + 128] = t[:, 512:640]
        t = dot(front, k["place_t"][:, 256 * ql : 256 * ql + 256]).astype(BF)
        for i, pair in enumerate(FRONT):
            j = BACK.index(pair)
            tc[64 * ql : 64 * ql + 64, 256 * i : 256 * i + 256] = t[64 * j : 64 * j + 64, :]

    load_vol.wait()
    loads["spread"].wait()

    def split_x(n, _):
        for parity in range(2):
            both = jnp.concatenate(
                [vol[:, 2 * zz + parity, pl.ds(16 * n, 16), :].reshape(512, 128) for zz in range(2)],
                axis=1)
            s = dot(both, k["spread"][...]).reshape(CI, 16, 384)
            for h in range(2):
                part = s[:, 8 * h : 8 * h + 8, :].reshape(256, 384).astype(BF)
                for e in range(3):
                    row = (3 * parity + e) * 256
                    vc[n, row : row + 256, 128 * h : 128 * h + 128] = part[:, 128 * e : 128 * e + 128]
        return 0

    lax.fori_loop(0, BANDS, split_x, 0)

    lane = lax.broadcasted_iota(jnp.int32, (256, 128), 1)

    def ft_copy(to, rows):
        return pltpu.make_async_remote_copy(
            src_ref=fs.at[to, 0:rows], dst_ref=rf.at[mg + 1, 0:rows],
            send_sem=ft_send.at[0], recv_sem=ft_recv.at[0],
            device_id=(mv, to), device_id_type=MESH)

    def forward(n, _):
        f01 = dot(tc[:, :1536], vc[n])
        f12 = dot(tc[:, 1536:], vc[n, 768:1536, :])
        for h in range(2):
            a, b = f01[:, 128 * h : 128 * h + 128], f12[:, 128 * h : 128 * h + 128]
            own = jnp.concatenate([a[0:64] + carry[0], a[64:256]], axis=0)
            late = jnp.concatenate([b[0:64] + carry[1], b[64:256]], axis=0)
            carry[0], carry[1] = a[256:320], b[256:320]
            swapped = pltpu.roll(late, 64, 1)
            total = own + jnp.where(lane >= 64, swapped, 0.0)
            for ql in range(4):
                q = 8 * n + 4 * h + ql
                low, high = swapped[64 * ql : 64 * ql + 32], late[64 * ql + 32 : 64 * ql + 64]
                fw[q] = total[64 * ql : 64 * ql + 64]
                fs[q, 64:96, :] = jnp.where(lane[0:32] < 64, low, high).astype(BF)
        return 0

    lax.fori_loop(0, BANDS, forward, 0)

    late_copy = pltpu.make_async_remote_copy(
        src_ref=fs.at[:, 64:96], dst_ref=late_in, send_sem=late_send.at[0], recv_sem=late_recv.at[0],
        device_id=(mv, mg + 1 - 2 * core), device_id_type=MESH)

    @pl.when(core == 0)
    def _():
        late_copy.start()

        def round_off(q, _):
            fs[q, 0:64] = fw[q].astype(BF)
            return 0

        lax.fori_loop(0, SLABS, round_off, 0)
        rf[mg + 1, 0:64] = fs[mg, 0:64]

    @pl.when(core == 1)
    def _():
        late_copy.wait_recv()

        def add_late(q, _):
            both = late_in[q].astype(F32)
            both = jnp.concatenate([both, pltpu.roll(both, 64, 1)], axis=0)
            fs[q, 0:64] = (fw[q] + jnp.where(lane[0:64] < 64, both, 0.0)).astype(BF)
            return 0

        lax.fori_loop(0, SLABS, add_late, 0)
        rf[mg + 1] = fs[mg]

    def send_ft(i, _):
        to = (mg + 5 * i) % SLABS

        @pl.when(core == 0)
        def _():
            ft_copy(to, 64).start()

        @pl.when(core == 1)
        def _():
            ft_copy(to, 96).start()

        return 0

    @pl.when(core == 0)
    def _():
        arrived(cr.at[0:31, 0:64], cot_recv)

    @pl.when(core == 1)
    def _():
        arrived(cr.at[0:31, 0:96], cot_recv)

    near_copy = pltpu.make_async_remote_copy(
        src_ref=near, dst_ref=cr.at[:, 64:96], send_sem=near_send.at[0], recv_sem=near_recv.at[0],
        device_id=(mv, mg + 1 - 2 * core), device_id_type=MESH)
    for name in ("squeeze", "shift", "later_lo", "later_hi"):
        loads[name].wait()

    @pl.when(core == 1)
    def _():
        def pass_on(n, _):
            rows = jnp.concatenate(
                [jnp.concatenate([cr[8 * n + i, 0:32], cr[8 * n + i, 32:64]], axis=1) for i in range(8)],
                axis=0)
            near[pl.ds(8 * n, 8)] = dot(rows, k["squeeze"][...]).astype(BF).reshape(8, 32, 128)
            return 0

        lax.fori_loop(0, BANDS, pass_on, 0)
        near_copy.start()

    lax.fori_loop(1, SLABS, send_ft, 0)

    def keep(n, h, ql, row, value):
        size = value.shape[0]
        c4[n + 1, 256 * ql + row : 256 * ql + row + size, 128 * h : 128 * h + 128] = value
        if ql == 0:
            c4[n + h, 1024 + row : 1024 + row + size, 128 * (1 - h) : 128 * (2 - h)] = value

    def forms_own(n, _):
        blocks = [cr[8 * n + i, 0:64] for i in range(8)]
        moved = dot(jnp.concatenate(blocks, axis=0), k["shift"][...]).astype(BF)
        for i in range(8):
            keep(n, i // 4, i % 4, 128, blocks[i])
            keep(n, i // 4, i % 4, 192, moved[64 * i : 64 * i + 64])
        return 0

    lax.fori_loop(0, BANDS, forms_own, 0)

    def forms_later(n, _):
        blocks = [cr[8 * n + i] for i in range(8)]
        for part_, name in ((0, "later_lo"), (1, "later_hi")):
            rows = jnp.concatenate(
                [jnp.concatenate([v[32 * part_ : 32 * part_ + 32], v[64:96]], axis=1) for v in blocks],
                axis=0)
            made = dot(rows, k[name][...]).astype(BF)
            for i in range(8):
                new = made[32 * i : 32 * i + 32]
                keep(n, i // 4, i % 4, 32 * part_, new[:, 0:128])
                keep(n, i // 4, i % 4, 64 + 32 * part_, new[:, 128:256])
        return 0

    yl = lax.broadcasted_iota(jnp.int32, (64, 256), 1) % 8

    def gradient(i, e):
        total = None
        start, taps = (64 if i == 2 else 128), 256 * (e + (0 if i == 0 else 3))
        for n in range(BANDS):
            rows = jnp.concatenate(
                [c4[n + 1, 256 * ql + start : 256 * ql + start + 64, :] for ql in range(5)], axis=0)
            term = dot_nt(rows, vc[n, taps : taps + 256, :])
            total = term if total is None else total + term
        g = [total[64 * ql : 64 * ql + 64] for ql in range(5)]
        d0 = jnp.where(yl == 1, g[1], jnp.where(yl == 3, g[2], jnp.where(
            yl == 5, g[3], jnp.where(yl == 7, g[4], 0.0))))
        rest = jnp.where(yl < 2, g[0], jnp.where(yl < 4, g[1], jnp.where(yl < 6, g[2], g[3])))
        d1, d2 = jnp.where(yl % 2 == 0, rest, 0.0), jnp.where(yl % 2 == 1, rest, 0.0)
        for b, d in enumerate((d0, d1, d2)):
            group, slot = divmod(9 * e + 3 * i + b, 4)
            at = (slice(64 * group, 64 * group + 64), slice(256 * slot, 256 * slot + 256))
            top = d.astype(BF)
            dh[at] = top
            dl[at] = (d - top.astype(F32)).astype(BF)

    for e in range(3):
        gradient(0, e)
        gradient(1, e)

    @pl.when(core == 0)
    def _():
        near_copy.wait_recv()

    lax.fori_loop(0, BANDS, forms_later, 0)
    for e in range(3):
        gradient(2, e)
    loads["bands"].wait()
    packed = dot(dh[...], k["bands"][...]) + dot(dl[...], k["bands"][...])
    terms[0:28] = packed.reshape(28, 16, 128)

    def layer_copy(source, target, send, recv, to, slot):
        return pltpu.make_async_remote_copy(
            src_ref=source, dst_ref=target.at[slot], send_sem=send.at[0], recv_sem=recv.at[0],
            device_id=(z_lo * 4 + to // 2 % 4, to // 8 * 8 + z_hi * 2 + to % 2), device_id_type=MESH)

    def part_copy(to, slot):
        return layer_copy(terms.at[to], part_in, part_send, part_recv, to, slot)

    def last_copy(to, slot):
        return layer_copy(whole, gathered, last_send, last_recv, to, slot)

    def whole_copy(to, slot):
        return pltpu.make_async_remote_copy(
            src_ref=part, dst_ref=whole_in.at[slot],
            send_sem=whole_send.at[0], recv_sem=whole_recv.at[0],
            device_id=(to % 2 * 4 + y, x * 8 + to // 2 * 2 + core), device_id_type=MESH)

    loads["weave"].wait()

    def backward(n):
        c = [c4[n + 1, 256 * ql : 256 * ql + 256, :] for ql in range(5)]
        oo = dot(tt_oo[...], c4[n + 1])
        oe = dot(tt_oe[...], jnp.concatenate([v[64:192] for v in c], axis=0))
        ev = dot(tt_e[...], jnp.concatenate([v[128:256] for v in c], axis=0))
        for parity, (at_even, at_odd) in enumerate(((ev[256:512], ev[0:256]), (oe, oo))):
            even, odd = at_even.astype(BF), at_odd.astype(BF)
            parts = []
            for h in range(2):
                lanes = slice(128 * h, 128 * h + 128)
                both = jnp.concatenate([even[:, lanes], odd[:, lanes]], axis=1)
                parts.append(dot(both, k["weave"][...]).reshape(CI, 8, 256))
            out = jnp.concatenate(parts, axis=1).astype(BF)
            for zz in range(2):
                vgrad[:, 2 * zz + parity, 16 * n : 16 * n + 16, :] = out[:, :, 128 * zz : 128 * zz + 128]

    def each(count, me, act):
        def step(i, _):
            act((me + i) % count)
            return 0

        lax.fori_loop(1, count, step, 0)

    each(32, mine, lambda to: part_copy(to, mine).start())
    part_in[mine] = terms[mine]

    @pl.when(core == 0)
    def _():
        late_copy.wait_send()
        arrived(vc.at[0, 0:1248], cot_send)

    @pl.when(core == 1)
    def _():
        near_copy.wait_send()
        arrived(vc.at[0, 0:1232], cot_send)

    backward(0)
    arrived(part_in.at[0:31], part_recv)
    part[...] = functools.reduce(jnp.add, [part_in[i] for i in range(32)])

    each(8, z, lambda to: whole_copy(to, z).start())
    whole_in[z] = part[...]
    arrived(terms.at[0:31], part_send)
    backward(1)
    arrived(whole_in.at[0:7], whole_recv)
    whole[...] = (functools.reduce(jnp.add, [whole_in[i] for i in range(8)]) * 0.125).astype(BF)

    each(32, mine, lambda to: last_copy(to, mine).start())
    gathered[mine] = whole[...]
    arrived(whole_in.at[0:7], whole_send)
    backward(2)
    backward(3)

    @pl.when(core == 0)
    def _():
        arrived(vc.at[0, 0:1248], ft_recv)
        arrived(fs.at[0:31, 0:64], ft_send)

    @pl.when(core == 1)
    def _():
        arrived(vc.at[0, 0:1232], ft_recv)
        arrived(fs.at[0:31, 0:96], ft_send)

    for name in ("join_lo", "join_hi", "unpick"):
        loads[name].wait()

    def unpack(m, _):
        for g in range(4):
            two = rf[pl.ds(8 * m + 1, 8), 16 * g : 16 * g + 16, :].reshape(128, 128)
            row = 64 + 16 * (g % 2)
            one = rf[pl.ds(8 * m, 8), row : row + 16, :].reshape(128, 128)
            summed = k["join_hi"] if g >= 2 else k["join_lo"]
            planes = dot(jnp.concatenate([two, one], axis=1), summed[...]).astype(BF)
            planes = jnp.concatenate([planes[:, 0:128], planes[:, 128:256]], axis=0)
            rows = dot(k["unpick"][...], planes)[:, 0:64].astype(BF)
            feat[16 * g : 16 * g + 16, pl.ds(16 * m, 16), :] = rows.reshape(16, 16, 64)
        return 0

    lax.fori_loop(0, 4, unpack, 0)

    arrived(gathered.at[0:31], last_recv)
    arrived(gathered.at[0:31], last_send)


def store(feat, vgrad, gathered, feat_out, vgrad_out, kgrad_out, kgrad, sem):
    copies = [
        pltpu.make_async_copy(source, target, sem.at[i])
        for i, (source, target) in enumerate(
            ((vgrad, vgrad_out), (feat, feat_out), (kgrad, kgrad_out)))
    ]
    copies[0].start()
    copies[1].start()
    for g in range(GROUPS):
        total = jnp.transpose(gathered[4 * g : 4 * g + 4].astype(F32).reshape(64, 128))
        for slot in range(4):
            if 4 * g + slot < len(TAPS):
                kgrad[TAPS[4 * g + slot]] = total[32 * slot : 32 * slot + 32]
    copies[2].start()
    for copy in copies:
        copy.wait()


def shards(volume, weights, cotangent):
    dma = pltpu.SemaphoreType.DMA
    outs = (
        jax.ShapeDtypeStruct((CO, 64, 64), BF),
        jax.ShapeDtypeStruct((CI, 4, 64, 128), BF),
        jax.ShapeDtypeStruct((3, 3, 3, CI, CO), F32),
    )
    held = (
        pltpu.VMEM((CO, 64, 64), BF),
        pltpu.VMEM((CI, 4, 64, 128), BF),
        pltpu.VMEM((32, 16, 128), BF),
    )
    scratch = [pltpu.VMEM(value.shape, BF) for _, value in CONSTANTS] + [
        pltpu.VMEM((CI, 4, 64, 128), BF),
        pltpu.VMEM((3, 3, 3, CI, CO), BF),
        pltpu.VMEM((CO, 64, 64), BF),
        pltpu.VMEM((SLABS + 1, 96, 128), BF),
        pltpu.VMEM((SLABS, 96, 128), BF),
        pltpu.VMEM((SLABS, 32, 128), BF),
        pltpu.VMEM((SLABS, 64, 128), F32),
        pltpu.VMEM((SLABS, 32, 128), BF),
        pltpu.VMEM((SLABS, 96, 128), BF),
        pltpu.VMEM((SLABS + 1, 96, 128), BF),
        pltpu.VMEM((128, 640), F32),
        pltpu.VMEM((QB, 9 * 256), BF),
        pltpu.VMEM((256, 1280), BF),
        pltpu.VMEM((256, 640), BF),
        pltpu.VMEM((512, 640), BF),
        pltpu.VMEM((BANDS, 1536, 256), BF),
        pltpu.VMEM((BANDS + 1, 1280, 256), BF),
        pltpu.VMEM((2, 64, 128), F32),
        pltpu.VMEM((64 * GROUPS, 1024), BF),
        pltpu.VMEM((64 * GROUPS, 1024), BF),
        pltpu.VMEM((32, 16, 128), F32),
        pltpu.VMEM((32, 16, 128), F32),
        pltpu.VMEM((16, 128), F32),
        pltpu.VMEM((8, 16, 128), F32),
        pltpu.VMEM((16, 128), BF),
        dma((3,)), dma((NC,)),
        *[dma((1,))] * 14,
    ]
    anywhere = pl.BlockSpec(memory_space=pltpu.HBM)
    inside = pl.BlockSpec(memory_space=pltpu.VMEM)
    results = pl.pallas_call(
        kernel,
        out_shape=held,
        in_specs=[anywhere] * (3 + NC),
        out_specs=(inside,) * 3,
        scratch_shapes=scratch,
        compiler_params=pltpu.CompilerParams(
            collective_id=0, has_side_effects=True, vmem_limit_bytes=40 << 20),
        cost_estimate=pl.CostEstimate(
            flops=2 * 10**10, bytes_accessed=8 << 20, transcendentals=0),
    )(*[
        pltpu.with_memory_space_constraint(value, pltpu.HBM)
        for value in (
            volume[0],
            jnp.transpose(weights, (2, 3, 4, 1, 0)),
            cotangent[0, :, :, 0, :],
            *[jnp.asarray(value) for _, value in CONSTANTS],
        )
    ])
    features, volume_grad, kernel_grad = pl.pallas_call(
        store,
        out_shape=outs,
        in_specs=[inside] * 3,
        out_specs=(anywhere,) * 3,
        scratch_shapes=[pltpu.VMEM((3, 3, 3, CI, CO), F32), dma((3,))],
        compiler_params=pltpu.CompilerParams(vmem_limit_bytes=8 << 20),
    )(*[pltpu.with_memory_space_constraint(value, pltpu.VMEM) for value in results])
    return (
        features[None, :, :, None, :],
        volume_grad[None],
        jnp.transpose(kernel_grad, (4, 3, 0, 1, 2)),
    )


def solution(mesh):
    placed = (P("vol", None, "gz", None, None), P(), P("vol", None, None, "gz", None))
    return jax.shard_map(
        shards,
        mesh=mesh,
        in_specs=placed,
        out_specs=(P("vol", None, None, "gz", None), P("vol", None, "gz", None, None), P()),
        check_vma=False,
    )
```

```python
import functools

import jax
import jax.numpy as jnp
import numpy as np
from jax import lax
from jax.experimental import pallas as pl
from jax.experimental.pallas import tpu as pltpu
from jax.sharding import PartitionSpec as P

MESH = pl.DeviceIdType.MESH
BF = jnp.bfloat16
F32 = jnp.float32

CI, CO, SLABS, BANDS = 32, 64, 32, 4
QB = 5 * CO

BACK = ((0, 0), (0, 2), (2, 2), (2, 0), (0, 1), (2, 1), (1, 2), (1, 0), (1, 1))
FRONT = ((1, 0), (1, 1), (1, 2), (2, 0), (2, 1), (2, 2), (0, 0), (0, 1), (0, 2))
TAPS = (
    *((a, b, e) for e in range(3) for a in (1, 2) for b in range(3)), None, None,
    *((0, b, e) for e in range(3) for b in range(3)), None, None, None,
)
GROUPS, FIRST = 8, 20


def one_hot(rows, columns, test):
    row, column = np.meshgrid(np.arange(rows), np.arange(columns), indexing="ij")
    return np.asarray(test(row, column), np.float32).astype(jnp.bfloat16)


def pair_pick(row, column):
    half, o, p = column // 256, column // 16 % 16, column % 16
    return (row % 16 == o) & (p == 2 * (row // 16) + half)


def even_pick(row, column):
    o, p = column // 16 % 16, column % 16
    return (row % 16 == o) & (p == 2 * (row // 16))


def unpick(row, column):
    half, slab, o = column // 128, column // 16 % 8, column % 16
    return (row // 16 == o) & (row % 16 == 2 * slab + half)


def place(row, column):
    ql, c, yl = row // 256, row // 8 % 32, row % 8
    b, channel = column // 32, column % 32
    return (b < 3) & (c == channel) & (yl == 2 * ql + b - 1)


def spread_x(row, column):
    zz, x = row // 128, row % 128
    e, half, r = column // 128, column // 64 % 2, column % 64
    return (zz == half) & (x == 2 * r + e - 1)


def weave_x(row, column):
    parity, zz, r = row // 128, row // 64 % 2, row % 64
    return (zz == column // 128) & (column % 128 == 2 * r + parity)


def shift_left(row, column):
    return (column % 64 < 63) & (row == column + 1)


def later_planes(high, row, column):
    shift = 1 - column // 128
    lane = column % 128 + shift
    valid = (column % 64 + shift) < 64
    return valid & (row == np.where(lane < 64, lane + 64, 128 + lane - (0 if high else 64)))


def squeeze(row, column):
    return (row // 128 == column // 64) & (row % 128 == column % 64)


def halves(row, column):
    return (column % 64 == row) & ((column // 64 == 0) | (column // 64 == 3))


def join(upper, row, column):
    even = (row == column) | (row == 128 + 64 * upper + column)
    odd = row == column - 64
    return np.where(column < 64, even, (column // 64 == 2) & odd)


def sum_band(row, column):
    return row // 8 == column


CONSTANTS = (
    ("halves", one_hot(64, 256, halves)),
    ("pairs", one_hot(128, 512, pair_pick)),
    ("evens", one_hot(128, 512, even_pick)),
    ("place", one_hot(5 * 256, 128, place)),
    ("place_t", np.ascontiguousarray(one_hot(5 * 256, 128, place).T)),
    ("spread", one_hot(256, 384, spread_x)),
    ("squeeze", one_hot(256, 128, squeeze)),
    ("shift", one_hot(128, 128, shift_left)),
    ("later_lo", one_hot(256, 256, functools.partial(later_planes, False))),
    ("later_hi", one_hot(256, 256, functools.partial(later_planes, True))),
    ("bands", one_hot(1024, 128, sum_band)),
    ("weave", one_hot(256, 256, weave_x)),
    ("join_lo", one_hot(256, 256, functools.partial(join, 0))),
    ("join_hi", one_hot(256, 256, functools.partial(join, 1))),
    ("unpick", one_hot(256, 256, unpick)),
)
NC = len(CONSTANTS)


def dot(a, b):
    return jnp.dot(a, b, preferred_element_type=F32)


def dot_nt(a, b):
    return lax.dot_general(a, b, (((1,), (1,)), ((), ())), preferred_element_type=F32)


def kernel(*refs):
    (vol_in, w_in, cot_in), refs = refs[:3], refs[3:]
    const_in, refs = refs[:NC], refs[NC:]
    (feat, vgrad, gathered), refs = refs[:3], refs[3:]
    const, refs = refs[:NC], refs[NC:]
    k = {name: ref for (name, _), ref in zip(CONSTANTS, const)}
    (vol, w, cot, cs, cr, near, fw, late_in, fs, rf, wa, tc, tt_oo, tt_oe, tt_e, vc, c4, carry,
     dh, dl, terms, part_in, part, whole_in, whole,
     in_sem, const_sem, cot_send, cot_recv, near_send, near_recv, late_send, late_recv,
     ft_send, ft_recv, part_send, part_recv, whole_send, whole_recv, last_send, last_recv) = refs

    mv, mg = lax.axis_index("vol"), lax.axis_index("gz")
    y, z_lo = mv % 4, mv // 4
    core, z_hi, x = mg % 2, mg // 2 % 4, mg // 8
    mine, z = x * 8 + y * 2 + core, z_hi * 2 + z_lo

    barrier = pltpu.get_barrier_semaphore()

    def greet(v, g):
        pl.semaphore_signal(barrier, inc=1, device_id=(v, g), device_id_type=MESH)

    def greet_slab(i, _):
        greet(mv, (mg + i) % SLABS)
        return 0

    lax.fori_loop(1, SLABS, greet_slab, 0)

    def greet_layer(i, _):
        greet(z_lo * 4 + (y + i // 8) % 4, (i % 8 // 2) * 8 + z_hi * 2 + i % 2)
        return 0

    lax.fori_loop(8, 32, greet_layer, 0)
    for other in range(4):
        greet((1 - z_lo) * 4 + y, x * 8 + other * 2 + core)

    load_cot = pltpu.make_async_copy(cot_in, cot, in_sem.at[0])
    load_w = pltpu.make_async_copy(w_in, w, in_sem.at[1])
    load_vol = pltpu.make_async_copy(vol_in, vol, in_sem.at[2])
    loads = {
        name: pltpu.make_async_copy(const_in[i], const[i], const_sem.at[i])
        for i, (name, _) in enumerate(CONSTANTS)
    }
    load_cot.start()
    for name in ("halves", "pairs", "evens"):
        loads[name].start()
    load_w.start()
    load_vol.start()
    for name in list(loads)[3:]:
        loads[name].start()

    cs[SLABS, 64:96, :] = jnp.zeros((32, 128), BF)
    rf[0, 64:96, :] = jnp.zeros((32, 128), BF)
    for slot in range(1, SLABS, 2):
        rf[slot, 64:96, :] = jnp.zeros((32, 128), BF)
    c4[BANDS, 1024:1280, 128:256] = jnp.zeros((256, 128), BF)
    for split in (dh, dl):
        split[256:320, 512:1024] = jnp.zeros((64, 512), BF)
        split[448:512, 256:1024] = jnp.zeros((64, 768), BF)
    carry[...] = jnp.zeros((2, 64, 128), F32)

    load_cot.wait()
    for name in ("halves", "pairs", "evens"):
        loads[name].wait()

    def pack(m, _):
        wide = []
        for g in range(4):
            block = cot[16 * g : 16 * g + 16, pl.ds(16 * m, 16), :].reshape(256, 64)
            wide.append(dot(block, k["halves"][...]).astype(BF))
        for g in range(4):
            both = jnp.concatenate([wide[g][:, :128], wide[g][:, 128:]], axis=0)
            two = dot(k["pairs"][...], both).astype(BF)
            cs[pl.ds(8 * m + 1, 8), 16 * g : 16 * g + 16, :] = two.reshape(8, 16, 128)
        for g in range(2):
            both = jnp.concatenate([wide[g][:, :128], wide[g + 2][:, 128:]], axis=0)
            two = dot(k["evens"][...], both).astype(BF)
            cs[pl.ds(8 * m, 8), 64 + 16 * g : 80 + 16 * g, :] = two.reshape(8, 16, 128)
        return 0

    lax.fori_loop(0, 4, pack, 0)

    pl.semaphore_wait(barrier, 59)

    def cot_copy(to, rows):
        return pltpu.make_async_remote_copy(
            src_ref=cs.at[to + 1, 0:rows], dst_ref=cr.at[mg, 0:rows],
            send_sem=cot_send.at[0], recv_sem=cot_recv.at[0],
            device_id=(mv, to), device_id_type=MESH)

    cr[mg, 0:64] = cs[mg + 1, 0:64]

    @pl.when(core == 1)
    def _():
        cr[mg, 64:96] = cs[mg + 1, 64:96]

    def send_cot(i, _):
        to = (mg + 5 * i) % SLABS

        @pl.when(to % 2 == 0)
        def _():
            cot_copy(to, 64).start()

        @pl.when(to % 2 == 1)
        def _():
            cot_copy(to, 96).start()

        return 0

    lax.fori_loop(1, SLABS, send_cot, 0)

    def arrived(buffer, sem):
        pltpu.make_async_copy(buffer, buffer, sem.at[0]).wait()

    load_w.wait()
    wa[...] = jnp.zeros((128, 640), F32)
    for b in range(3):
        for i in range(0, 10, 2):
            (a, e), rows = BACK[i], slice(32 * b, 32 * b + 32)
            first = w[a, b, e].astype(F32)
            if i + 1 < 9:
                a, e = BACK[i + 1]
                second = w[a, b, e].astype(F32)
            else:
                second = jnp.zeros((32, 64), F32)
            wa[rows, 64 * i : 64 * i + 128] = jnp.concatenate([first, second], axis=1)
    for name in ("place", "place_t"):
        loads[name].wait()
    taps = wa[...]
    back = taps.astype(BF)
    front = jnp.transpose(taps).astype(BF)
    for ql in range(5):
        t = dot(k["place"][256 * ql : 256 * ql + 256, :], back).astype(BF)
        tt_oo[:, 256 * ql : 256 * ql + 256] = t[:, 0:256]
        tt_oe[:, 128 * ql : 128 * ql + 128] = t[:, 256:384]
        tt_e[0:256, 128 * ql : 128 * ql + 128] = t[:, 384:512]
        tt_e[256:512, 128 * ql : 128 * ql + 128] = t[:, 512:640]
        t = dot(front, k["place_t"][:, 256 * ql : 256 * ql + 256]).astype(BF)
        for i, pair in enumerate(FRONT):
            j = BACK.index(pair)
            tc[64 * ql : 64 * ql + 64, 256 * i : 256 * i + 256] = t[64 * j : 64 * j + 64, :]

    load_vol.wait()
    loads["spread"].wait()

    def split_x(n, _):
        for parity in range(2):
            both = jnp.concatenate(
                [vol[:, 2 * zz + parity, pl.ds(16 * n, 16), :].reshape(512, 128) for zz in range(2)],
                axis=1)
            s = dot(both, k["spread"][...]).reshape(CI, 16, 384)
            for h in range(2):
                part = s[:, 8 * h : 8 * h + 8, :].reshape(256, 384).astype(BF)
                for e in range(3):
                    row = (3 * parity + e) * 256
                    vc[n, row : row + 256, 128 * h : 128 * h + 128] = part[:, 128 * e : 128 * e + 128]
        return 0

    lax.fori_loop(0, BANDS, split_x, 0)

    lane = lax.broadcasted_iota(jnp.int32, (256, 128), 1)

    def ft_copy(to, rows):
        return pltpu.make_async_remote_copy(
            src_ref=fs.at[to, 0:rows], dst_ref=rf.at[mg + 1, 0:rows],
            send_sem=ft_send.at[0], recv_sem=ft_recv.at[0],
            device_id=(mv, to), device_id_type=MESH)

    def forward(n, _):
        f01 = dot(tc[:, :1536], vc[n])
        f12 = dot(tc[:, 1536:], vc[n, 768:1536, :])
        for h in range(2):
            a, b = f01[:, 128 * h : 128 * h + 128], f12[:, 128 * h : 128 * h + 128]
            own = jnp.concatenate([a[0:64] + carry[0], a[64:256]], axis=0)
            late = jnp.concatenate([b[0:64] + carry[1], b[64:256]], axis=0)
            carry[0], carry[1] = a[256:320], b[256:320]
            swapped = pltpu.roll(late, 64, 1)
            total = own + jnp.where(lane >= 64, swapped, 0.0)
            for ql in range(4):
                q = 8 * n + 4 * h + ql
                low, high = swapped[64 * ql : 64 * ql + 32], late[64 * ql + 32 : 64 * ql + 64]
                fw[q] = total[64 * ql : 64 * ql + 64]
                fs[q, 64:96, :] = jnp.where(lane[0:32] < 64, low, high).astype(BF)
        return 0

    lax.fori_loop(0, BANDS, forward, 0)

    late_copy = pltpu.make_async_remote_copy(
        src_ref=fs.at[:, 64:96], dst_ref=late_in, send_sem=late_send.at[0], recv_sem=late_recv.at[0],
        device_id=(mv, mg + 1 - 2 * core), device_id_type=MESH)

    @pl.when(core == 0)
    def _():
        late_copy.start()

        def round_off(q, _):
            fs[q, 0:64] = fw[q].astype(BF)
            return 0

        lax.fori_loop(0, SLABS, round_off, 0)
        rf[mg + 1, 0:64] = fs[mg, 0:64]

    @pl.when(core == 1)
    def _():
        late_copy.wait_recv()

        def add_late(q, _):
            both = late_in[q].astype(F32)
            both = jnp.concatenate([both, pltpu.roll(both, 64, 1)], axis=0)
            fs[q, 0:64] = (fw[q] + jnp.where(lane[0:64] < 64, both, 0.0)).astype(BF)
            return 0

        lax.fori_loop(0, SLABS, add_late, 0)
        rf[mg + 1] = fs[mg]

    def send_ft(i, _):
        to = (mg + 5 * i) % SLABS

        @pl.when(core == 0)
        def _():
            ft_copy(to, 64).start()

        @pl.when(core == 1)
        def _():
            ft_copy(to, 96).start()

        return 0

    @pl.when(core == 0)
    def _():
        arrived(cr.at[0:31, 0:64], cot_recv)

    @pl.when(core == 1)
    def _():
        arrived(cr.at[0:31, 0:96], cot_recv)

    near_copy = pltpu.make_async_remote_copy(
        src_ref=near, dst_ref=cr.at[:, 64:96], send_sem=near_send.at[0], recv_sem=near_recv.at[0],
        device_id=(mv, mg + 1 - 2 * core), device_id_type=MESH)
    for name in ("squeeze", "shift", "later_lo", "later_hi"):
        loads[name].wait()

    @pl.when(core == 1)
    def _():
        def pass_on(n, _):
            rows = jnp.concatenate(
                [jnp.concatenate([cr[8 * n + i, 0:32], cr[8 * n + i, 32:64]], axis=1) for i in range(8)],
                axis=0)
            near[pl.ds(8 * n, 8)] = dot(rows, k["squeeze"][...]).astype(BF).reshape(8, 32, 128)
            return 0

        lax.fori_loop(0, BANDS, pass_on, 0)
        near_copy.start()

    lax.fori_loop(1, SLABS, send_ft, 0)

    def keep(n, h, ql, row, value):
        size = value.shape[0]
        c4[n + 1, 256 * ql + row : 256 * ql + row + size, 128 * h : 128 * h + 128] = value
        if ql == 0:
            c4[n + h, 1024 + row : 1024 + row + size, 128 * (1 - h) : 128 * (2 - h)] = value

    def forms_own(n, _):
        blocks = [cr[8 * n + i, 0:64] for i in range(8)]
        moved = dot(jnp.concatenate(blocks, axis=0), k["shift"][...]).astype(BF)
        for i in range(8):
            keep(n, i // 4, i % 4, 128, blocks[i])
            keep(n, i // 4, i % 4, 192, moved[64 * i : 64 * i + 64])
        return 0

    lax.fori_loop(0, BANDS, forms_own, 0)

    def forms_later(n, _):
        blocks = [cr[8 * n + i] for i in range(8)]
        for part_, name in ((0, "later_lo"), (1, "later_hi")):
            rows = jnp.concatenate(
                [jnp.concatenate([v[32 * part_ : 32 * part_ + 32], v[64:96]], axis=1) for v in blocks],
                axis=0)
            made = dot(rows, k[name][...]).astype(BF)
            for i in range(8):
                new = made[32 * i : 32 * i + 32]
                keep(n, i // 4, i % 4, 32 * part_, new[:, 0:128])
                keep(n, i // 4, i % 4, 64 + 32 * part_, new[:, 128:256])
        return 0

    def layer_copy(source, target, send, recv, to, slot):
        return pltpu.make_async_remote_copy(
            src_ref=source, dst_ref=target.at[slot], send_sem=send.at[0], recv_sem=recv.at[0],
            device_id=(z_lo * 4 + to // 2 % 4, to // 8 * 8 + z_hi * 2 + to % 2), device_id_type=MESH)

    def part_copy(to, slot):
        return layer_copy(terms.at[to], part_in, part_send, part_recv, to, slot)

    def last_copy(to, slot):
        return layer_copy(whole, gathered, last_send, last_recv, to, slot)

    def whole_copy(to, slot):
        return pltpu.make_async_remote_copy(
            src_ref=part, dst_ref=whole_in.at[slot],
            send_sem=whole_send.at[0], recv_sem=whole_recv.at[0],
            device_id=(to % 2 * 4 + y, x * 8 + to // 2 * 2 + core), device_id_type=MESH)

    def each(count, me, act):
        def step(i, _):
            act((me + i) % count)
            return 0

        lax.fori_loop(1, count, step, 0)

    yl = lax.broadcasted_iota(jnp.int32, (64, 256), 1) % 8

    def gradient(i, e):
        total = None
        start, taps = (64 if i == 2 else 128), 256 * (e + (0 if i == 0 else 3))
        for n in range(BANDS):
            rows = jnp.concatenate(
                [c4[n + 1, 256 * ql + start : 256 * ql + start + 64, :] for ql in range(5)], axis=0)
            term = dot_nt(rows, vc[n, taps : taps + 256, :])
            total = term if total is None else total + term
        g = [total[64 * ql : 64 * ql + 64] for ql in range(5)]
        d0 = jnp.where(yl == 1, g[1], jnp.where(yl == 3, g[2], jnp.where(
            yl == 5, g[3], jnp.where(yl == 7, g[4], 0.0))))
        rest = jnp.where(yl < 2, g[0], jnp.where(yl < 4, g[1], jnp.where(yl < 6, g[2], g[3])))
        d1, d2 = jnp.where(yl % 2 == 0, rest, 0.0), jnp.where(yl % 2 == 1, rest, 0.0)
        for b, d in enumerate((d0, d1, d2)):
            group, slot = divmod(6 * e + 3 * i + b if i < 2 else FIRST + 3 * e + b, 4)
            at = (slice(64 * group, 64 * group + 64), slice(256 * slot, 256 * slot + 256))
            top = d.astype(BF)
            dh[at] = top
            dl[at] = (d - top.astype(F32)).astype(BF)

    for e in range(3):
        gradient(0, e)
        gradient(1, e)
    loads["bands"].wait()

    def send_parts(first, end):
        rows = slice(16 * first, 16 * end)
        packed = dot(dh[rows], k["bands"][...]) + dot(dl[rows], k["bands"][...])
        terms[first:end] = packed.reshape(end - first, 16, 128)

        def send(to):
            @pl.when((to >= first) & (to < end))
            def _():
                part_copy(to, mine).start()

        each(32, mine, send)

    send_parts(0, FIRST)

    @pl.when(core == 0)
    def _():
        near_copy.wait_recv()

    lax.fori_loop(0, BANDS, forms_later, 0)
    for e in range(3):
        gradient(2, e)
    send_parts(FIRST, 32)

    loads["weave"].wait()

    def backward(n):
        c = [c4[n + 1, 256 * ql : 256 * ql + 256, :] for ql in range(5)]
        oo = dot(tt_oo[...], c4[n + 1])
        oe = dot(tt_oe[...], jnp.concatenate([v[64:192] for v in c], axis=0))
        ev = dot(tt_e[...], jnp.concatenate([v[128:256] for v in c], axis=0))
        for parity, (at_even, at_odd) in enumerate(((ev[256:512], ev[0:256]), (oe, oo))):
            even, odd = at_even.astype(BF), at_odd.astype(BF)
            parts = []
            for h in range(2):
                lanes = slice(128 * h, 128 * h + 128)
                both = jnp.concatenate([even[:, lanes], odd[:, lanes]], axis=1)
                parts.append(dot(both, k["weave"][...]).reshape(CI, 8, 256))
            out = jnp.concatenate(parts, axis=1).astype(BF)
            for zz in range(2):
                vgrad[:, 2 * zz + parity, 16 * n : 16 * n + 16, :] = out[:, :, 128 * zz : 128 * zz + 128]

    part_in[mine] = terms[mine]

    @pl.when(core == 0)
    def _():
        late_copy.wait_send()
        arrived(vc.at[0, 0:1248], cot_send)

    @pl.when(core == 1)
    def _():
        near_copy.wait_send()
        arrived(vc.at[0, 0:1232], cot_send)

    backward(0)
    arrived(part_in.at[0:31], part_recv)
    part[...] = functools.reduce(jnp.add, [part_in[i] for i in range(32)])

    each(8, z, lambda to: whole_copy(to, z).start())
    whole_in[z] = part[...]
    arrived(terms.at[0:31], part_send)
    backward(1)
    arrived(whole_in.at[0:7], whole_recv)
    whole[...] = (functools.reduce(jnp.add, [whole_in[i] for i in range(8)]) * 0.125).astype(BF)

    each(32, mine, lambda to: last_copy(to, mine).start())
    gathered[mine] = whole[...]
    arrived(whole_in.at[0:7], whole_send)
    backward(2)
    backward(3)

    @pl.when(core == 0)
    def _():
        arrived(vc.at[0, 0:1248], ft_recv)
        arrived(fs.at[0:31, 0:64], ft_send)

    @pl.when(core == 1)
    def _():
        arrived(vc.at[0, 0:1232], ft_recv)
        arrived(fs.at[0:31, 0:96], ft_send)

    for name in ("join_lo", "join_hi", "unpick"):
        loads[name].wait()

    def unpack(m, _):
        for g in range(4):
            two = rf[pl.ds(8 * m + 1, 8), 16 * g : 16 * g + 16, :].reshape(128, 128)
            row = 64 + 16 * (g % 2)
            one = rf[pl.ds(8 * m, 8), row : row + 16, :].reshape(128, 128)
            summed = k["join_hi"] if g >= 2 else k["join_lo"]
            planes = dot(jnp.concatenate([two, one], axis=1), summed[...]).astype(BF)
            planes = jnp.concatenate([planes[:, 0:128], planes[:, 128:256]], axis=0)
            rows = dot(k["unpick"][...], planes)[:, 0:64].astype(BF)
            feat[16 * g : 16 * g + 16, pl.ds(16 * m, 16), :] = rows.reshape(16, 16, 64)
        return 0

    lax.fori_loop(0, 4, unpack, 0)

    arrived(gathered.at[0:31], last_recv)
    arrived(gathered.at[0:31], last_send)


def store(feat, vgrad, gathered, feat_out, vgrad_out, kgrad_out, kgrad, sem):
    copies = [
        pltpu.make_async_copy(source, target, sem.at[i])
        for i, (source, target) in enumerate(
            ((vgrad, vgrad_out), (feat, feat_out), (kgrad, kgrad_out)))
    ]
    copies[0].start()
    copies[1].start()
    for g in range(GROUPS):
        total = jnp.transpose(gathered[4 * g : 4 * g + 4].astype(F32).reshape(64, 128))
        for slot in range(4):
            if TAPS[4 * g + slot] is not None:
                kgrad[TAPS[4 * g + slot]] = total[32 * slot : 32 * slot + 32]
    copies[2].start()
    for copy in copies:
        copy.wait()


def shards(volume, weights, cotangent):
    dma = pltpu.SemaphoreType.DMA
    outs = (
        jax.ShapeDtypeStruct((CO, 64, 64), BF),
        jax.ShapeDtypeStruct((CI, 4, 64, 128), BF),
        jax.ShapeDtypeStruct((3, 3, 3, CI, CO), F32),
    )
    held = (
        pltpu.VMEM((CO, 64, 64), BF),
        pltpu.VMEM((CI, 4, 64, 128), BF),
        pltpu.VMEM((32, 16, 128), BF),
    )
    scratch = [pltpu.VMEM(value.shape, BF) for _, value in CONSTANTS] + [
        pltpu.VMEM((CI, 4, 64, 128), BF),
        pltpu.VMEM((3, 3, 3, CI, CO), BF),
        pltpu.VMEM((CO, 64, 64), BF),
        pltpu.VMEM((SLABS + 1, 96, 128), BF),
        pltpu.VMEM((SLABS, 96, 128), BF),
        pltpu.VMEM((SLABS, 32, 128), BF),
        pltpu.VMEM((SLABS, 64, 128), F32),
        pltpu.VMEM((SLABS, 32, 128), BF),
        pltpu.VMEM((SLABS, 96, 128), BF),
        pltpu.VMEM((SLABS + 1, 96, 128), BF),
        pltpu.VMEM((128, 640), F32),
        pltpu.VMEM((QB, 9 * 256), BF),
        pltpu.VMEM((256, 1280), BF),
        pltpu.VMEM((256, 640), BF),
        pltpu.VMEM((512, 640), BF),
        pltpu.VMEM((BANDS, 1536, 256), BF),
        pltpu.VMEM((BANDS + 1, 1280, 256), BF),
        pltpu.VMEM((2, 64, 128), F32),
        pltpu.VMEM((64 * GROUPS, 1024), BF),
        pltpu.VMEM((64 * GROUPS, 1024), BF),
        pltpu.VMEM((32, 16, 128), F32),
        pltpu.VMEM((32, 16, 128), F32),
        pltpu.VMEM((16, 128), F32),
        pltpu.VMEM((8, 16, 128), F32),
        pltpu.VMEM((16, 128), BF),
        dma((3,)), dma((NC,)),
        *[dma((1,))] * 14,
    ]
    anywhere = pl.BlockSpec(memory_space=pltpu.HBM)
    inside = pl.BlockSpec(memory_space=pltpu.VMEM)
    results = pl.pallas_call(
        kernel,
        out_shape=held,
        in_specs=[anywhere] * (3 + NC),
        out_specs=(inside,) * 3,
        scratch_shapes=scratch,
        compiler_params=pltpu.CompilerParams(
            collective_id=0, has_side_effects=True, vmem_limit_bytes=40 << 20),
        cost_estimate=pl.CostEstimate(
            flops=2 * 10**10, bytes_accessed=8 << 20, transcendentals=0),
    )(*[
        pltpu.with_memory_space_constraint(value, pltpu.HBM)
        for value in (
            volume[0],
            jnp.transpose(weights, (2, 3, 4, 1, 0)),
            cotangent[0, :, :, 0, :],
            *[jnp.asarray(value) for _, value in CONSTANTS],
        )
    ])
    features, volume_grad, kernel_grad = pl.pallas_call(
        store,
        out_shape=outs,
        in_specs=[inside] * 3,
        out_specs=(anywhere,) * 3,
        scratch_shapes=[pltpu.VMEM((3, 3, 3, CI, CO), F32), dma((3,))],
        compiler_params=pltpu.CompilerParams(vmem_limit_bytes=8 << 20),
    )(*[pltpu.with_memory_space_constraint(value, pltpu.VMEM) for value in results])
    return (
        features[None, :, :, None, :],
        volume_grad[None],
        jnp.transpose(kernel_grad, (4, 3, 0, 1, 2)),
    )


def solution(mesh):
    placed = (P("vol", None, "gz", None, None), P(), P("vol", None, None, "gz", None))
    return jax.shard_map(
        shards,
        mesh=mesh,
        in_specs=placed,
        out_specs=(P("vol", None, None, "gz", None), P("vol", None, "gz", None, None), P()),
        check_vma=False,
    )
```

```python
import functools

import jax
import jax.numpy as jnp
import numpy as np
from jax import lax
from jax.experimental import pallas as pl
from jax.experimental.pallas import tpu as pltpu
from jax.sharding import PartitionSpec as P

MESH = pl.DeviceIdType.MESH
BF = jnp.bfloat16
F32 = jnp.float32

CI, CO, SLABS, BANDS = 32, 64, 32, 4
QB = 5 * CO

BACK = ((0, 0), (0, 2), (2, 2), (2, 0), (0, 1), (2, 1), (1, 2), (1, 0), (1, 1))
FRONT = ((1, 0), (1, 1), (1, 2), (2, 0), (2, 1), (2, 2), (0, 0), (0, 1), (0, 2))
TAPS = tuple((a, b, e) for e in range(3) for a in (1, 2, 0) for b in range(3))
GROUPS = 7


def one_hot(rows, columns, test):
    row, column = np.meshgrid(np.arange(rows), np.arange(columns), indexing="ij")
    return np.asarray(test(row, column), np.float32).astype(jnp.bfloat16)


def pair_pick(row, column):
    half, o, p = column // 256, column // 16 % 16, column % 16
    return (row % 16 == o) & (p == 2 * (row // 16) + half)


def even_pick(row, column):
    o, p = column // 16 % 16, column % 16
    return (row % 16 == o) & (p == 2 * (row // 16))


def unpick(row, column):
    half, slab, o = column // 128, column // 16 % 8, column % 16
    return (row // 16 == o) & (row % 16 == 2 * slab + half)


def place(row, column):
    ql, c, yl = row // 256, row // 8 % 32, row % 8
    b, channel = column // 32, column % 32
    return (b < 3) & (c == channel) & (yl == 2 * ql + b - 1)


def spread_x(row, column):
    zz, x = row // 128, row % 128
    e, half, r = column // 128, column // 64 % 2, column % 64
    return (zz == half) & (x == 2 * r + e - 1)


def weave_x(row, column):
    parity, zz, r = row // 128, row // 64 % 2, row % 64
    return (zz == column // 128) & (column % 128 == 2 * r + parity)


def shift_left(row, column):
    return (column % 64 < 63) & (row == column + 1)


def later_planes(high, row, column):
    shift = 1 - column // 128
    lane = column % 128 + shift
    valid = (column % 64 + shift) < 64
    return valid & (row == np.where(lane < 64, lane + 64, 128 + lane - (0 if high else 64)))


def squeeze(row, column):
    return (row // 128 == column // 64) & (row % 128 == column % 64)


def halves(row, column):
    return (column % 64 == row) & ((column // 64 == 0) | (column // 64 == 3))


def join(upper, row, column):
    even = (row == column) | (row == 128 + 64 * upper + column)
    odd = row == column - 64
    return np.where(column < 64, even, (column // 64 == 2) & odd)


def sum_band(row, column):
    return row // 8 == column


CONSTANTS = (
    ("halves", one_hot(64, 256, halves)),
    ("pairs", one_hot(128, 512, pair_pick)),
    ("evens", one_hot(128, 512, even_pick)),
    ("place", one_hot(5 * 256, 128, place)),
    ("place_t", np.ascontiguousarray(one_hot(5 * 256, 128, place).T)),
    ("spread", one_hot(256, 384, spread_x)),
    ("squeeze", one_hot(256, 128, squeeze)),
    ("shift", one_hot(128, 128, shift_left)),
    ("later_lo", one_hot(256, 256, functools.partial(later_planes, False))),
    ("later_hi", one_hot(256, 256, functools.partial(later_planes, True))),
    ("bands", one_hot(1024, 128, sum_band)),
    ("weave", one_hot(256, 256, weave_x)),
    ("join_lo", one_hot(256, 256, functools.partial(join, 0))),
    ("join_hi", one_hot(256, 256, functools.partial(join, 1))),
    ("unpick", one_hot(256, 256, unpick)),
)
NC = len(CONSTANTS)


def dot(a, b):
    return jnp.dot(a, b, preferred_element_type=F32)


def dot_nt(a, b):
    return lax.dot_general(a, b, (((1,), (1,)), ((), ())), preferred_element_type=F32)


def kernel(*refs):
    (vol_in, w_in, cot_in), refs = refs[:3], refs[3:]
    const_in, refs = refs[:NC], refs[NC:]
    (feat, vgrad, gathered), refs = refs[:3], refs[3:]
    const, refs = refs[:NC], refs[NC:]
    k = {name: ref for (name, _), ref in zip(CONSTANTS, const)}
    (vol, w, cot, cs, cr, near, fw, late_in, fs, rf, wa, tc, tt_oo, tt_oe, tt_e, vc, c4, carry,
     dh, dl, terms, part_in, part, whole_in, whole,
     in_sem, const_sem, cot_send, cot_recv, near_send, near_recv, late_send, late_recv,
     ft_send, ft_recv, part_send, part_recv, whole_send, whole_recv, last_send, last_recv) = refs

    mv, mg = lax.axis_index("vol"), lax.axis_index("gz")
    y, z_lo = mv % 4, mv // 4
    core, z_hi, x = mg % 2, mg // 2 % 4, mg // 8
    mine, z = x * 8 + y * 2 + core, z_hi * 2 + z_lo

    barrier = pltpu.get_barrier_semaphore()

    def greet(v, g):
        pl.semaphore_signal(barrier, inc=1, device_id=(v, g), device_id_type=MESH)

    def greet_slab(i, _):
        greet(mv, (mg + i) % SLABS)
        return 0

    lax.fori_loop(1, SLABS, greet_slab, 0)

    def greet_layer(i, _):
        greet(z_lo * 4 + (y + i // 8) % 4, (i % 8 // 2) * 8 + z_hi * 2 + i % 2)
        return 0

    lax.fori_loop(8, 32, greet_layer, 0)
    for other in range(4):
        greet((1 - z_lo) * 4 + y, x * 8 + other * 2 + core)

    load_cot = pltpu.make_async_copy(cot_in, cot, in_sem.at[0])
    load_w = pltpu.make_async_copy(w_in, w, in_sem.at[1])
    load_vol = pltpu.make_async_copy(vol_in, vol, in_sem.at[2])
    loads = {
        name: pltpu.make_async_copy(const_in[i], const[i], const_sem.at[i])
        for i, (name, _) in enumerate(CONSTANTS)
    }
    load_cot.start()
    for name in ("halves", "pairs", "evens"):
        loads[name].start()
    load_w.start()
    load_vol.start()
    for name in list(loads)[3:]:
        loads[name].start()

    cs[SLABS, 64:96, :] = jnp.zeros((32, 128), BF)
    rf[0, 64:96, :] = jnp.zeros((32, 128), BF)
    for slot in range(1, SLABS, 2):
        rf[slot, 64:96, :] = jnp.zeros((32, 128), BF)
    c4[BANDS, 1024:1280, 128:256] = jnp.zeros((256, 128), BF)
    dh[384:448, 768:1024] = jnp.zeros((64, 256), BF)
    dl[384:448, 768:1024] = jnp.zeros((64, 256), BF)
    terms[28:32] = jnp.zeros((4, 16, 128), F32)
    carry[...] = jnp.zeros((2, 64, 128), F32)

    load_cot.wait()
    for name in ("halves", "pairs", "evens"):
        loads[name].wait()

    def pack(m, _):
        wide = []
        for g in range(4):
            block = cot[16 * g : 16 * g + 16, pl.ds(16 * m, 16), :].reshape(256, 64)
            wide.append(dot(block, k["halves"][...]).astype(BF))
        for g in range(4):
            both = jnp.concatenate([wide[g][:, :128], wide[g][:, 128:]], axis=0)
            two = dot(k["pairs"][...], both).astype(BF)
            cs[pl.ds(8 * m + 1, 8), 16 * g : 16 * g + 16, :] = two.reshape(8, 16, 128)
        for g in range(2):
            both = jnp.concatenate([wide[g][:, :128], wide[g + 2][:, 128:]], axis=0)
            two = dot(k["evens"][...], both).astype(BF)
            cs[pl.ds(8 * m, 8), 64 + 16 * g : 80 + 16 * g, :] = two.reshape(8, 16, 128)
        return 0

    lax.fori_loop(0, 4, pack, 0)

    pl.semaphore_wait(barrier, 59)

    def cot_copy(to, rows):
        return pltpu.make_async_remote_copy(
            src_ref=cs.at[to + 1, 0:rows], dst_ref=cr.at[mg, 0:rows],
            send_sem=cot_send.at[0], recv_sem=cot_recv.at[0],
            device_id=(mv, to), device_id_type=MESH)

    cr[mg, 0:64] = cs[mg + 1, 0:64]

    @pl.when(core == 1)
    def _():
        cr[mg, 64:96] = cs[mg + 1, 64:96]

    def send_cot(i, _):
        to = (mg + 5 * i) % SLABS

        @pl.when(to % 2 == 0)
        def _():
            cot_copy(to, 64).start()

        @pl.when(to % 2 == 1)
        def _():
            cot_copy(to, 96).start()

        return 0

    lax.fori_loop(1, SLABS, send_cot, 0)

    def arrived(buffer, sem):
        pltpu.make_async_copy(buffer, buffer, sem.at[0]).wait()

    load_w.wait()
    wa[...] = jnp.zeros((128, 640), F32)
    for b in range(3):
        for i in range(0, 10, 2):
            (a, e), rows = BACK[i], slice(32 * b, 32 * b + 32)
            first = w[a, b, e].astype(F32)
            if i + 1 < 9:
                a, e = BACK[i + 1]
                second = w[a, b, e].astype(F32)
            else:
                second = jnp.zeros((32, 64), F32)
            wa[rows, 64 * i : 64 * i + 128] = jnp.concatenate([first, second], axis=1)
    for name in ("place", "place_t"):
        loads[name].wait()
    taps = wa[...]
    back = taps.astype(BF)
    front = jnp.transpose(taps).astype(BF)
    for ql in range(5):
        t = dot(k["place"][256 * ql : 256 * ql + 256, :], back).astype(BF)
        tt_oo[:, 256 * ql : 256 * ql + 256] = t[:, 0:256]
        tt_oe[:, 128 * ql : 128 * ql + 128] = t[:, 256:384]
        tt_e[0:256, 128 * ql : 128 * ql + 128] = t[:, 384:512]
        tt_e[256:512, 128 * ql : 128 * ql + 128] = t[:, 512:640]
        t = dot(front, k["place_t"][:, 256 * ql : 256 * ql + 256]).astype(BF)
        for i, pair in enumerate(FRONT):
            j = BACK.index(pair)
            tc[64 * ql : 64 * ql + 64, 256 * i : 256 * i + 256] = t[64 * j : 64 * j + 64, :]

    load_vol.wait()
    loads["spread"].wait()

    def split_x(n, _):
        for parity in range(2):
            both = jnp.concatenate(
                [vol[:, 2 * zz + parity, pl.ds(16 * n, 16), :].reshape(512, 128) for zz in range(2)],
                axis=1)
            s = dot(both, k["spread"][...]).reshape(CI, 16, 384)
            for h in range(2):
                part = s[:, 8 * h : 8 * h + 8, :].reshape(256, 384).astype(BF)
                for e in range(3):
                    row = (3 * parity + e) * 256
                    vc[n, row : row + 256, 128 * h : 128 * h + 128] = part[:, 128 * e : 128 * e + 128]
        return 0

    lax.fori_loop(0, BANDS, split_x, 0)

    lane = lax.broadcasted_iota(jnp.int32, (256, 128), 1)

    def ft_copy(to, rows):
        return pltpu.make_async_remote_copy(
            src_ref=fs.at[to, 0:rows], dst_ref=rf.at[mg + 1, 0:rows],
            send_sem=ft_send.at[0], recv_sem=ft_recv.at[0],
            device_id=(mv, to), device_id_type=MESH)

    def forward(n, _):
        f01 = dot(tc[:, :1536], vc[n])
        f12 = dot(tc[:, 1536:], vc[n, 768:1536, :])
        for h in range(2):
            a, b = f01[:, 128 * h : 128 * h + 128], f12[:, 128 * h : 128 * h + 128]
            own = jnp.concatenate([a[0:64] + carry[0], a[64:256]], axis=0)
            late = jnp.concatenate([b[0:64] + carry[1], b[64:256]], axis=0)
            carry[0], carry[1] = a[256:320], b[256:320]
            swapped = pltpu.roll(late, 64, 1)
            total = own + jnp.where(lane >= 64, swapped, 0.0)
            for ql in range(4):
                q = 8 * n + 4 * h + ql
                low, high = swapped[64 * ql : 64 * ql + 32], late[64 * ql + 32 : 64 * ql + 64]
                fw[q] = total[64 * ql : 64 * ql + 64]
                fs[q, 64:96, :] = jnp.where(lane[0:32] < 64, low, high).astype(BF)
        return 0

    lax.fori_loop(0, BANDS, forward, 0)

    late_copy = pltpu.make_async_remote_copy(
        src_ref=fs.at[:, 64:96], dst_ref=late_in, send_sem=late_send.at[0], recv_sem=late_recv.at[0],
        device_id=(mv, mg + 1 - 2 * core), device_id_type=MESH)

    @pl.when(core == 0)
    def _():
        late_copy.start()

        def round_off(q, _):
            fs[q, 0:64] = fw[q].astype(BF)
            return 0

        lax.fori_loop(0, SLABS, round_off, 0)
        rf[mg + 1, 0:64] = fs[mg, 0:64]

    @pl.when(core == 1)
    def _():
        late_copy.wait_recv()

        def add_late(q, _):
            both = late_in[q].astype(F32)
            both = jnp.concatenate([both, pltpu.roll(both, 64, 1)], axis=0)
            fs[q, 0:64] = (fw[q] + jnp.where(lane[0:64] < 64, both, 0.0)).astype(BF)
            return 0

        lax.fori_loop(0, SLABS, add_late, 0)
        rf[mg + 1] = fs[mg]

    def send_ft(i, _):
        to = (mg + 5 * i) % SLABS

        @pl.when(core == 0)
        def _():
            ft_copy(to, 64).start()

        @pl.when(core == 1)
        def _():
            ft_copy(to, 96).start()

        return 0

    @pl.when(core == 0)
    def _():
        arrived(cr.at[0:31, 0:64], cot_recv)

    @pl.when(core == 1)
    def _():
        arrived(cr.at[0:31, 0:96], cot_recv)

    near_copy = pltpu.make_async_remote_copy(
        src_ref=near, dst_ref=cr.at[:, 64:96], send_sem=near_send.at[0], recv_sem=near_recv.at[0],
        device_id=(mv, mg + 1 - 2 * core), device_id_type=MESH)
    for name in ("squeeze", "shift", "later_lo", "later_hi"):
        loads[name].wait()

    @pl.when(core == 1)
    def _():
        def pass_on(n, _):
            rows = jnp.concatenate(
                [jnp.concatenate([cr[8 * n + i, 0:32], cr[8 * n + i, 32:64]], axis=1) for i in range(8)],
                axis=0)
            near[pl.ds(8 * n, 8)] = dot(rows, k["squeeze"][...]).astype(BF).reshape(8, 32, 128)
            return 0

        lax.fori_loop(0, BANDS, pass_on, 0)
        near_copy.start()

    lax.fori_loop(1, SLABS, send_ft, 0)

    def keep(n, h, ql, row, value):
        size = value.shape[0]
        c4[n + 1, 256 * ql + row : 256 * ql + row + size, 128 * h : 128 * h + 128] = value
        if ql == 0:
            c4[n + h, 1024 + row : 1024 + row + size, 128 * (1 - h) : 128 * (2 - h)] = value

    def forms_own(n, _):
        blocks = [cr[8 * n + i, 0:64] for i in range(8)]
        moved = dot(jnp.concatenate(blocks, axis=0), k["shift"][...]).astype(BF)
        for i in range(8):
            keep(n, i // 4, i % 4, 128, blocks[i])
            keep(n, i // 4, i % 4, 192, moved[64 * i : 64 * i + 64])
        return 0

    lax.fori_loop(0, BANDS, forms_own, 0)

    def forms_later(n, _):
        blocks = [cr[8 * n + i] for i in range(8)]
        for part_, name in ((0, "later_lo"), (1, "later_hi")):
            rows = jnp.concatenate(
                [jnp.concatenate([v[32 * part_ : 32 * part_ + 32], v[64:96]], axis=1) for v in blocks],
                axis=0)
            made = dot(rows, k[name][...]).astype(BF)
            for i in range(8):
                new = made[32 * i : 32 * i + 32]
                keep(n, i // 4, i % 4, 32 * part_, new[:, 0:128])
                keep(n, i // 4, i % 4, 64 + 32 * part_, new[:, 128:256])
        return 0

    yl = lax.broadcasted_iota(jnp.int32, (64, 256), 1) % 8

    def gradient(i, e):
        total = None
        start, taps = (64 if i == 2 else 128), 256 * (e + (0 if i == 0 else 3))
        for n in range(BANDS):
            rows = jnp.concatenate(
                [c4[n + 1, 256 * ql + start : 256 * ql + start + 64, :] for ql in range(5)], axis=0)
            term = dot_nt(rows, vc[n, taps : taps + 256, :])
            total = term if total is None else total + term
        g = [total[64 * ql : 64 * ql + 64] for ql in range(5)]
        d0 = jnp.where(yl == 1, g[1], jnp.where(yl == 3, g[2], jnp.where(
            yl == 5, g[3], jnp.where(yl == 7, g[4], 0.0))))
        rest = jnp.where(yl < 2, g[0], jnp.where(yl < 4, g[1], jnp.where(yl < 6, g[2], g[3])))
        d1, d2 = jnp.where(yl % 2 == 0, rest, 0.0), jnp.where(yl % 2 == 1, rest, 0.0)
        for b, d in enumerate((d0, d1, d2)):
            group, slot = divmod(9 * e + 3 * i + b, 4)
            at = (slice(64 * group, 64 * group + 64), slice(256 * slot, 256 * slot + 256))
            top = d.astype(BF)
            dh[at] = top
            dl[at] = (d - top.astype(F32)).astype(BF)

    for e in range(3):
        gradient(0, e)
        gradient(1, e)

    @pl.when(core == 0)
    def _():
        near_copy.wait_recv()

    lax.fori_loop(0, BANDS, forms_later, 0)
    for e in range(3):
        gradient(2, e)
    loads["bands"].wait()
    packed = dot(dh[...], k["bands"][...]) + dot(dl[...], k["bands"][...])
    terms[0:28] = packed.reshape(28, 16, 128)

    def layer_copy(source, target, send, recv, to, slot):
        return pltpu.make_async_remote_copy(
            src_ref=source, dst_ref=target.at[slot], send_sem=send.at[0], recv_sem=recv.at[0],
            device_id=(z_lo * 4 + to // 2 % 4, to // 8 * 8 + z_hi * 2 + to % 2), device_id_type=MESH)

    def part_copy(to, slot):
        return layer_copy(terms.at[to], part_in, part_send, part_recv, to, slot)

    def last_copy(to, slot):
        return layer_copy(whole, gathered, last_send, last_recv, to, slot)

    def whole_copy(to, slot):
        return pltpu.make_async_remote_copy(
            src_ref=part, dst_ref=whole_in.at[slot],
            send_sem=whole_send.at[0], recv_sem=whole_recv.at[0],
            device_id=(to % 2 * 4 + y, x * 8 + to // 2 * 2 + core), device_id_type=MESH)

    loads["weave"].wait()

    def backward(n):
        c = [c4[n + 1, 256 * ql : 256 * ql + 256, :] for ql in range(5)]
        oo = dot(tt_oo[...], c4[n + 1])
        oe = dot(tt_oe[...], jnp.concatenate([v[64:192] for v in c], axis=0))
        ev = dot(tt_e[...], jnp.concatenate([v[128:256] for v in c], axis=0))
        for parity, (at_even, at_odd) in enumerate(((ev[256:512], ev[0:256]), (oe, oo))):
            even, odd = at_even.astype(BF), at_odd.astype(BF)
            parts = []
            for h in range(2):
                lanes = slice(128 * h, 128 * h + 128)
                both = jnp.concatenate([even[:, lanes], odd[:, lanes]], axis=1)
                parts.append(dot(both, k["weave"][...]).reshape(CI, 8, 256))
            out = jnp.concatenate(parts, axis=1).astype(BF)
            for zz in range(2):
                vgrad[:, 2 * zz + parity, 16 * n : 16 * n + 16, :] = out[:, :, 128 * zz : 128 * zz + 128]

    def each(count, me, act):
        def step(i, _):
            act((me + i) % count)
            return 0

        lax.fori_loop(1, count, step, 0)

    each(32, mine, lambda to: part_copy(to, mine).start())
    part_in[mine] = terms[mine]

    @pl.when(core == 0)
    def _():
        late_copy.wait_send()
        arrived(vc.at[0, 0:1248], cot_send)

    @pl.when(core == 1)
    def _():
        near_copy.wait_send()
        arrived(vc.at[0, 0:1232], cot_send)

    backward(0)
    backward(1)
    arrived(part_in.at[0:31], part_recv)
    part[...] = functools.reduce(jnp.add, [part_in[i] for i in range(32)])

    each(8, z, lambda to: whole_copy(to, z).start())
    whole_in[z] = part[...]
    arrived(terms.at[0:31], part_send)
    backward(2)
    backward(3)
    arrived(whole_in.at[0:7], whole_recv)
    whole[...] = (functools.reduce(jnp.add, [whole_in[i] for i in range(8)]) * 0.125).astype(BF)

    each(32, mine, lambda to: last_copy(to, mine).start())
    gathered[mine] = whole[...]
    arrived(whole_in.at[0:7], whole_send)

    @pl.when(core == 0)
    def _():
        arrived(vc.at[0, 0:1248], ft_recv)
        arrived(fs.at[0:31, 0:64], ft_send)

    @pl.when(core == 1)
    def _():
        arrived(vc.at[0, 0:1232], ft_recv)
        arrived(fs.at[0:31, 0:96], ft_send)

    for name in ("join_lo", "join_hi", "unpick"):
        loads[name].wait()

    def unpack(m, _):
        for g in range(4):
            two = rf[pl.ds(8 * m + 1, 8), 16 * g : 16 * g + 16, :].reshape(128, 128)
            row = 64 + 16 * (g % 2)
            one = rf[pl.ds(8 * m, 8), row : row + 16, :].reshape(128, 128)
            summed = k["join_hi"] if g >= 2 else k["join_lo"]
            planes = dot(jnp.concatenate([two, one], axis=1), summed[...]).astype(BF)
            planes = jnp.concatenate([planes[:, 0:128], planes[:, 128:256]], axis=0)
            rows = dot(k["unpick"][...], planes)[:, 0:64].astype(BF)
            feat[16 * g : 16 * g + 16, pl.ds(16 * m, 16), :] = rows.reshape(16, 16, 64)
        return 0

    lax.fori_loop(0, 4, unpack, 0)

    arrived(gathered.at[0:31], last_recv)
    arrived(gathered.at[0:31], last_send)


def store(feat, vgrad, gathered, feat_out, vgrad_out, kgrad_out, kgrad, sem):
    copies = [
        pltpu.make_async_copy(source, target, sem.at[i])
        for i, (source, target) in enumerate(
            ((vgrad, vgrad_out), (feat, feat_out), (kgrad, kgrad_out)))
    ]
    copies[0].start()
    copies[1].start()
    for g in range(GROUPS):
        total = jnp.transpose(gathered[4 * g : 4 * g + 4].astype(F32).reshape(64, 128))
        for slot in range(4):
            if 4 * g + slot < len(TAPS):
                kgrad[TAPS[4 * g + slot]] = total[32 * slot : 32 * slot + 32]
    copies[2].start()
    for copy in copies:
        copy.wait()


def shards(volume, weights, cotangent):
    dma = pltpu.SemaphoreType.DMA
    outs = (
        jax.ShapeDtypeStruct((CO, 64, 64), BF),
        jax.ShapeDtypeStruct((CI, 4, 64, 128), BF),
        jax.ShapeDtypeStruct((3, 3, 3, CI, CO), F32),
    )
    held = (
        pltpu.VMEM((CO, 64, 64), BF),
        pltpu.VMEM((CI, 4, 64, 128), BF),
        pltpu.VMEM((32, 16, 128), BF),
    )
    scratch = [pltpu.VMEM(value.shape, BF) for _, value in CONSTANTS] + [
        pltpu.VMEM((CI, 4, 64, 128), BF),
        pltpu.VMEM((3, 3, 3, CI, CO), BF),
        pltpu.VMEM((CO, 64, 64), BF),
        pltpu.VMEM((SLABS + 1, 96, 128), BF),
        pltpu.VMEM((SLABS, 96, 128), BF),
        pltpu.VMEM((SLABS, 32, 128), BF),
        pltpu.VMEM((SLABS, 64, 128), F32),
        pltpu.VMEM((SLABS, 32, 128), BF),
        pltpu.VMEM((SLABS, 96, 128), BF),
        pltpu.VMEM((SLABS + 1, 96, 128), BF),
        pltpu.VMEM((128, 640), F32),
        pltpu.VMEM((QB, 9 * 256), BF),
        pltpu.VMEM((256, 1280), BF),
        pltpu.VMEM((256, 640), BF),
        pltpu.VMEM((512, 640), BF),
        pltpu.VMEM((BANDS, 1536, 256), BF),
        pltpu.VMEM((BANDS + 1, 1280, 256), BF),
        pltpu.VMEM((2, 64, 128), F32),
        pltpu.VMEM((64 * GROUPS, 1024), BF),
        pltpu.VMEM((64 * GROUPS, 1024), BF),
        pltpu.VMEM((32, 16, 128), F32),
        pltpu.VMEM((32, 16, 128), F32),
        pltpu.VMEM((16, 128), F32),
        pltpu.VMEM((8, 16, 128), F32),
        pltpu.VMEM((16, 128), BF),
        dma((3,)), dma((NC,)),
        *[dma((1,))] * 14,
    ]
    anywhere = pl.BlockSpec(memory_space=pltpu.HBM)
    inside = pl.BlockSpec(memory_space=pltpu.VMEM)
    results = pl.pallas_call(
        kernel,
        out_shape=held,
        in_specs=[anywhere] * (3 + NC),
        out_specs=(inside,) * 3,
        scratch_shapes=scratch,
        compiler_params=pltpu.CompilerParams(
            collective_id=0, has_side_effects=True, vmem_limit_bytes=40 << 20),
        cost_estimate=pl.CostEstimate(
            flops=2 * 10**10, bytes_accessed=8 << 20, transcendentals=0),
    )(*[
        pltpu.with_memory_space_constraint(value, pltpu.HBM)
        for value in (
            volume[0],
            jnp.transpose(weights, (2, 3, 4, 1, 0)),
            cotangent[0, :, :, 0, :],
            *[jnp.asarray(value) for _, value in CONSTANTS],
        )
    ])
    features, volume_grad, kernel_grad = pl.pallas_call(
        store,
        out_shape=outs,
        in_specs=[inside] * 3,
        out_specs=(anywhere,) * 3,
        scratch_shapes=[pltpu.VMEM((3, 3, 3, CI, CO), F32), dma((3,))],
        compiler_params=pltpu.CompilerParams(vmem_limit_bytes=8 << 20),
    )(*[pltpu.with_memory_space_constraint(value, pltpu.VMEM) for value in results])
    return (
        features[None, :, :, None, :],
        volume_grad[None],
        jnp.transpose(kernel_grad, (4, 3, 0, 1, 2)),
    )


def solution(mesh):
    placed = (P("vol", None, "gz", None, None), P(), P("vol", None, None, "gz", None))
    return jax.shard_map(
        shards,
        mesh=mesh,
        in_specs=placed,
        out_specs=(P("vol", None, None, "gz", None), P("vol", None, "gz", None, None), P()),
        check_vma=False,
    )
```
